512 devices in a mesh: wide: 128 (over y, z, core), narrow: 4 (over x).
Axes of the slice: x: 4, y: 8, z: 8, core: 2. Of those that a mesh axis runs over, the one named last changes fastest.
Arguments:
- tokens: bfloat16 [65536, 2048], P(('wide', 'narrow')), may hold values from -6 to 6
- route_slot: int32 [65536, 2], P(('wide', 'narrow')), may hold values from 0 to 2, all different within a row
- route_code: int32 [65536, 2], P(('wide', 'narrow')), may hold values from 1 to 255
- group_hits: int32 [128, 3], replicated, may hold values from 0 to 127, as said below
- gate_w: bfloat16 [2048, 384, 128], P('wide', 'narrow'), may hold values from -0.125 to 0.125
- up_w: bfloat16 [2048, 384, 128], P('wide', 'narrow'), may hold values from -0.125 to 0.125
- down_w: bfloat16 [2048, 384, 128], P('wide', 'narrow'), may hold values from -0.3125 to 0.3125
- gate_scale: bfloat16 [2048, 128], P('wide'), may hold values from 0.5 to 2
- up_scale: bfloat16 [2048, 128], P('wide'), may hold values from 0.5 to 2
- down_scale: bfloat16 [2048, 128], P('wide'), may hold values from 0.5 to 2
- cotangent: bfloat16 [65536, 2048], P(('wide', 'narrow')), may hold values from -6 to 6
Outputs:
- mixed: bfloat16 [65536, 2048], P(('wide', 'narrow'))
- token_grad: bfloat16 [65536, 2048], P(('wide', 'narrow'))
- gate_grad: bfloat16 [2048, 384, 128], P('wide', 'narrow')
- up_grad: bfloat16 [2048, 384, 128], P('wide', 'narrow')
- down_grad: bfloat16 [2048, 384, 128], P('wide', 'narrow')
The draws below stay inside these ranges and needn't reach their ends.
Inputs may be any that keep to these rules, and one draw needn't show every extreme that they name: `group_hits`: row g names 3 different experts, and every expert is named in exactly 3 rows. `route_slot`: each row names 2 different slots.
All inputs are finite; a program needn't handle non-finite values.
Results may differ from the reference program's by a relative error of at most 0.013.
Values may be sent and summed in bfloat16 or wider, within the bound.
No kernel may reach another device: no remote copies, remote signals or barrier semaphores. Data moves between devices by JAX's collectives and lax.ppermute only.
A program may use at most 128 MiB of HBM per device.

```python
import math
import jax
import jax.numpy as jnp
from jax import lax

D = 2048
FF = 384
HITS = 3
TOPK = 2
TOK_DEV = 128
EXPERTS = 128
GROUPS = 128
TOKENS = 65536
N_NARROW = 4


def draw_group_hits(key, part):
    key = jax.random.fold_in(key, 11)
    first, second = jax.random.split(key)
    order = jax.random.permutation(first, EXPERTS)
    offsets = jax.random.permutation(second, EXPERTS)[:HITS]
    groups = jnp.arange(GROUPS, dtype=jnp.int32)[:, None]
    return order[(groups + offsets[None, :]) % EXPERTS].astype(jnp.int32)


def plant(values, stream_key, smallest, largest):
    shape = values.shape
    place = [jax.random.randint(jax.random.fold_in(stream_key, axis), (), 0, shape[axis]) for axis in range(len(shape))]
    values = values.at[tuple(place)].set(smallest)
    longest = shape.index(max(shape))
    place[longest] = (place[longest] + 1) % shape[longest]
    return values.at[tuple(place)].set(largest)


def shard_levels(key, extent, shards, smallest, high):
    loudness = 1.0
    for dim, blocks in shards:
        steps = jax.random.uniform(jax.random.fold_in(jax.random.fold_in(key, 6), dim), (blocks,), jnp.float32, smallest / len(shards), high / len(shards))
        loudness = loudness * jnp.repeat(jnp.exp(steps), extent[dim] // blocks).reshape((-1,) + (1,) * (len(extent) - 1 - dim))
    return loudness


def picks_of(rng, rows, number_of, top, lift):
    order = jax.random.permutation(jax.random.fold_in(rng, 1), number_of)
    favour = order
    for power in range(3):
        favour = favour * favour // number_of
    favour = favour * lift // number_of
    chance = jax.random.randint(jax.random.fold_in(rng, 2), (rows, number_of), 0, 4096) + favour
    sure = jax.random.permutation(jax.random.fold_in(rng, 3), rows)[jnp.arange(number_of) % rows]
    chance = jnp.where(jnp.arange(rows)[:, None] == sure[None, :], 1 << 14, chance)
    merit = chance * number_of + jnp.arange(number_of)
    return lax.top_k(merit.astype(jnp.int32), top)[1].astype(jnp.int32)


def noise(key, shape, width, limit, shards=(), held_as=jnp.bfloat16):
    result = width * jax.random.normal(key, shape, jnp.float32)
    if shards:
        result = result * shard_levels(key, shape, shards, -0.22, 0.18)
    return jnp.clip(result, -limit, limit).astype(held_as)


def setup_inputs(seed: int = 0) -> dict:
    seeds = jax.random.split(jax.random.key(seed), 12)
    return {
        "tokens": noise(seeds[0], (TOKENS, D), 1.0, 6.0, ((0, 512),)),
        "route_slot": picks_of(seeds[1], TOKENS, HITS, TOPK, 5461),
        "route_code": plant(jax.random.randint(seeds[2], (TOKENS, TOPK), 1, 256), jax.random.fold_in(seeds[2], 1), 1, 255).astype(jnp.int32),
        "group_hits": draw_group_hits(jax.random.fold_in(seeds[11], 71), 0),
        "gate_w": noise(seeds[4], (D, FF, EXPERTS), D ** -0.5, 0.125, ((0, 128), (1, 4))),
        "up_w": noise(seeds[5], (D, FF, EXPERTS), D ** -0.5, 0.125, ((0, 128), (1, 4))),
        "down_w": noise(seeds[6], (D, FF, EXPERTS), FF ** -0.5, 0.3125, ((0, 128), (1, 4))),
        "gate_scale": jnp.clip(jnp.exp(math.log(2.0) - 1.3862944 * jax.random.uniform(seeds[7], (D, EXPERTS), jnp.float32) ** shard_levels(seeds[7], (D, EXPERTS), ((0, 128),), -0.2, 0.2)), 0.5, 2.0).astype(jnp.bfloat16),
        "up_scale": jnp.clip(jnp.exp(math.log(2.0) - 1.3862944 * jax.random.uniform(seeds[8], (D, EXPERTS), jnp.float32) ** shard_levels(seeds[8], (D, EXPERTS), ((0, 128),), -0.2, 0.2)), 0.5, 2.0).astype(jnp.bfloat16),
        "down_scale": jnp.clip(jnp.exp(math.log(2.0) - 1.3862944 * jax.random.uniform(seeds[9], (D, EXPERTS), jnp.float32) ** shard_levels(seeds[9], (D, EXPERTS), ((0, 128),), -0.2, 0.2)), 0.5, 2.0).astype(jnp.bfloat16),
        "cotangent": noise(seeds[10], (TOKENS, D), 1.0, 6.0, ((0, 512),)),
    }


def dequant(weight, scale, hits):
    picked = weight[:, :, hits].astype(jnp.float32) * scale[:, hits].astype(jnp.float32)[:, None, :]
    return jnp.transpose(picked.astype(jnp.bfloat16), (0, 2, 1))


def split_sum(pairs, count):
    block = FF // N_NARROW
    total = None
    for left, right in pairs:
        first = left.astype(jnp.float32).reshape(count, HITS, N_NARROW, block)
        second = right.astype(jnp.float32).reshape(D, HITS, N_NARROW, block)
        term = jnp.einsum('tkbf,dkbf->btd', first, second)
        total = term if total is None else total + term
    parts = lax.optimization_barrier(total.astype(jnp.bfloat16))
    return jnp.sum(parts.astype(jnp.float32), axis=0).astype(jnp.bfloat16)


def reference(tokens, route_slot, route_code, group_hits, gate_w, up_w, down_w, gate_scale, up_scale, down_scale, cotangent):
    codes = route_code.astype(jnp.float32)
    shares = codes / jnp.sum(codes, axis=1, keepdims=True)
    picked = (route_slot[:, :, None] == jnp.arange(HITS, dtype=jnp.int32)[None, None, :]).astype(jnp.float32)
    rweight = jnp.sum(picked * shares[:, :, None], axis=1).astype(jnp.bfloat16)
    count = TOK_DEV * N_NARROW

    def one_group(carry, index):
        acc_gate, acc_up, acc_down = carry
        hits = group_hits[index]
        start = (index * count).astype(jnp.int32)
        inputs = lax.dynamic_slice_in_dim(tokens, start, count, 0)
        upstream = lax.dynamic_slice_in_dim(cotangent, start, count, 0)
        weights = lax.dynamic_slice_in_dim(rweight, start, count, 0).astype(jnp.float32)[:, :, None]
        w_gate = dequant(gate_w, gate_scale, hits)
        w_up = dequant(up_w, up_scale, hits)
        w_down = dequant(down_w, down_scale, hits)
        inputs_f = inputs.astype(jnp.float32)
        upstream_f = upstream.astype(jnp.float32)
        gate = jnp.einsum('td,dkf->tkf', inputs_f, w_gate.astype(jnp.float32))
        up = jnp.einsum('td,dkf->tkf', inputs_f, w_up.astype(jnp.float32))
        sig = jax.nn.sigmoid(gate)
        silu = gate * sig
        weighted = (weights * silu * up).astype(jnp.bfloat16)
        mixed = split_sum([(weighted, w_down)], count)
        d_weighted = jnp.einsum('td,dkf->tkf', upstream_f, w_down.astype(jnp.float32))
        d_act = weights * d_weighted
        d_gate = (d_act * up * sig * (1.0 + gate * (1.0 - sig))).astype(jnp.bfloat16)
        d_up = (d_act * silu).astype(jnp.bfloat16)
        term_down = jnp.einsum('td,tkf->dfk', upstream_f, weighted.astype(jnp.float32)).astype(jnp.bfloat16)
        term_gate = jnp.einsum('td,tkf->dfk', inputs_f, d_gate.astype(jnp.float32)).astype(jnp.bfloat16)
        term_up = jnp.einsum('td,tkf->dfk', inputs_f, d_up.astype(jnp.float32)).astype(jnp.bfloat16)
        token_grad = split_sum([(d_gate, w_gate), (d_up, w_up)], count)
        acc_gate = acc_gate.at[:, :, hits].add(term_gate.astype(jnp.float32))
        acc_up = acc_up.at[:, :, hits].add(term_up.astype(jnp.float32))
        acc_down = acc_down.at[:, :, hits].add(term_down.astype(jnp.float32))
        return (acc_gate, acc_up, acc_down), (mixed, token_grad)

    empty = jnp.zeros((D, FF, EXPERTS), jnp.float32)
    totals, outputs = lax.scan(one_group, (empty, empty, empty), jnp.arange(GROUPS, dtype=jnp.int32))
    mixed = outputs[0].reshape(TOKENS, D)
    token_grad = outputs[1].reshape(TOKENS, D)
    return (mixed, token_grad, totals[0].astype(jnp.bfloat16), totals[1].astype(jnp.bfloat16), totals[2].astype(jnp.bfloat16))
```

```python
import jax
import jax.numpy as jnp
from jax import lax
from jax.experimental import pallas as pl
from jax.experimental.pallas import tpu as pltpu
from jax.sharding import PartitionSpec as P

LANES = 128
VMEM_LIMIT = 56 * 1024 * 1024


def lane_index(shape):
    return lax.broadcasted_iota(jnp.int32, shape, len(shape) - 1)


def pack_kernel(hits_ref, gate_ref, up_ref, down_ref, gs_ref, us_ref, ds_ref, out_ref, held, wide):
    rows, block, experts = gate_ref.shape
    groups = out_ref.shape[0]
    for m, (w_ref, s_ref) in enumerate(((gate_ref, gs_ref), (up_ref, us_ref), (down_ref, ds_ref))):
        wide[...] = s_ref[...].astype(jnp.float32)

        @pl.loop(0, rows)
        def _(r, m=m, w_ref=w_ref):
            scale = wide[pl.ds(r, 1), :]
            scaled = w_ref[r].astype(jnp.float32) * scale
            scaled = scaled.astype(jnp.bfloat16).astype(jnp.float32)
            full = jnp.concatenate([scaled, jnp.zeros((LANES - block, experts), jnp.float32)], axis=0)
            start = pl.multiple_of((m * rows + r) * experts, experts)
            held[pl.ds(start, experts), :] = full.T

    lane = lane_index((rows, LANES))

    @pl.loop(0, groups, unroll=2)
    def _(g):
        tail = jnp.zeros((rows, LANES), jnp.float32)
        for m in range(3):
            part = [
                held[pl.ds(m * rows * experts + hits_ref[3 * g + k], rows, stride=experts), :]
                for k in range(3)
            ]
            second = pltpu.roll(part[1], 96, 1)
            third = pltpu.roll(part[2], 64, 1)
            out_ref[g, :, 256 * m : 256 * m + 128] = jnp.where(lane < 96, part[0], second).astype(jnp.bfloat16)
            out_ref[g, :, 256 * m + 128 : 256 * m + 256] = jnp.where(lane < 64, second, third).astype(jnp.bfloat16)
            ext = third if m == 0 else part[2] if m == 2 else pltpu.roll(part[2], 96, 1)
            tail = jnp.where((lane >= 32 * m) & (lane < 32 * m + 32), ext, tail)
        out_ref[g, :, 768:896] = tail.astype(jnp.bfloat16)


def settle_kernel(hits_ref, recv_ref, gate_ref, up_ref, down_ref, acc):
    rows, block, experts = gate_ref.shape
    groups = recv_ref.shape[0]
    acc[...] = jnp.zeros_like(acc)

    @pl.loop(0, groups)
    def _(g):
        spots = [hits_ref[3 * g + k] * rows for k in range(3)]
        tail = recv_ref[g, :, 768:896].astype(jnp.float32)
        lane = lane_index((rows, LANES))
        terms = []
        for m in range(3):
            low = recv_ref[g, :, 256 * m : 256 * m + 128].astype(jnp.float32)
            high = recv_ref[g, :, 256 * m + 128 : 256 * m + 256].astype(jnp.float32)
            second = pltpu.roll(jnp.where(lane < 64, high, low), 32, 1)
            third = pltpu.roll(high, 64, 1)
            ext = tail if m == 2 else pltpu.roll(tail, 64 - 32 * m, 1)
            third = jnp.where(lane < 64, third, ext)
            terms.append((low, second, third))
        old = [
            [acc[m, pl.ds(pl.multiple_of(spots[k], rows), rows), :] for k in range(3)] for m in range(3)
        ]
        for m in range(3):
            for k in range(3):
                acc[m, pl.ds(pl.multiple_of(spots[k], rows), rows), :] = old[m][k] + terms[m][k]

    for m, out_ref in enumerate((gate_ref, up_ref, down_ref)):

        @pl.loop(0, rows)
        def _(r, m=m, out_ref=out_ref):
            mine = acc[m, pl.ds(r, experts, stride=rows), :]
            out_ref[r] = mine.T[:block].astype(jnp.bfloat16)


def dot(left, right):
    return lax.dot_general(left, right, (((1,), (0,)), ((), ())), preferred_element_type=jnp.float32)


def dot_t(left, right):
    return lax.dot_general(left, right, (((1,), (1,)), ((), ())), preferred_element_type=jnp.float32)


def middle_kernel(x_ref, dy_ref, xt_ref, dyt_ref, rw_ref, w_ref, term_ref, act_ref):
    tok = x_ref.shape[0]
    width = x_ref.shape[1]
    chunk = 256

    @pl.loop(0, tok // chunk)
    def _(i):
        rows = pl.ds(pl.multiple_of(i * chunk, chunk), chunk)
        gate = dot(x_ref[rows, :], w_ref[:, 0:256])
        up = dot(x_ref[rows, :], w_ref[:, 256:512])
        back = dot(dy_ref[rows, :], w_ref[:, 512:768])
        tail_x = dot(x_ref[rows, :], w_ref[:, 768:896])
        tail_dy = dot(dy_ref[rows, :], w_ref[:, 768:896])
        rw = rw_ref[rows, :].astype(jnp.float32)
        lane = lane_index((chunk, 256))
        main_rw = jnp.where(lane < 96, rw[:, 0:1], jnp.where(lane < 192, rw[:, 1:2], rw[:, 2:3]))

        def finish(gate, up, back, share):
            sig = jax.nn.sigmoid(gate)
            silu = gate * sig
            weighted = share * silu * up
            d_act = share * back
            d_gate = d_act * up * sig * (1.0 + gate * (1.0 - sig))
            return d_gate, d_act * silu, weighted

        d_gate, d_up, weighted = finish(gate, up, back, main_rw)
        act_ref[rows, 0:256] = d_gate.astype(jnp.bfloat16)
        act_ref[rows, 256:512] = d_up.astype(jnp.bfloat16)
        act_ref[rows, 512:768] = weighted.astype(jnp.bfloat16)
        d_gate, d_up, weighted = finish(
            tail_x, pltpu.roll(tail_x, 96, 1), pltpu.roll(tail_dy, 64, 1), rw[:, 2:3]
        )
        lane = lane_index((chunk, LANES))
        from_x = jnp.where(lane < 32, d_gate, jnp.where(lane < 64, pltpu.roll(d_up, 32, 1), 0.0))
        from_dy = jnp.where((lane >= 64) & (lane < 96), pltpu.roll(weighted, 64, 1), 0.0)
        act_ref[rows, 768:896] = from_x.astype(jnp.bfloat16)
        act_ref[rows, 896:1024] = from_dy.astype(jnp.bfloat16)

    @pl.loop(0, width // 512)
    def _(i):
        cols = pl.ds(pl.multiple_of(i * 512, 512), 512)
        xt = xt_ref[cols, :]
        dyt = dyt_ref[cols, :]
        term_ref[cols, 0:256] = dot(xt, act_ref[:, 0:256]).astype(jnp.bfloat16)
        term_ref[cols, 256:512] = dot(xt, act_ref[:, 256:512]).astype(jnp.bfloat16)
        term_ref[cols, 512:768] = dot(dyt, act_ref[:, 512:768]).astype(jnp.bfloat16)
        tail = dot(xt, act_ref[:, 768:896]) + dot(dyt, act_ref[:, 896:1024])
        term_ref[cols, 768:896] = tail.astype(jnp.bfloat16)


def out_kernel(act_ref, w_ref, mixed_ref, grad_ref):
    width = w_ref.shape[0]

    @pl.loop(0, width // 512)
    def _(i):
        cols = pl.ds(pl.multiple_of(i * 512, 512), 512)
        tail = w_ref[cols, 768:896]
        mixed = dot_t(act_ref[:, 512:768], w_ref[cols, 512:768]) + dot_t(act_ref[:, 896:1024], tail)
        mixed_ref[:, cols] = mixed.astype(jnp.bfloat16)
        grad = dot_t(act_ref[:, 0:512], w_ref[cols, 0:512]) + dot_t(act_ref[:, 768:896], tail)
        grad_ref[:, cols] = grad.astype(jnp.bfloat16)


def flip_kernel(x_ref, dy_ref, xt_ref, dyt_ref):
    @pl.loop(0, x_ref.shape[1] // 512)
    def _(i):
        cols = pl.ds(pl.multiple_of(i * 512, 512), 512)
        xt_ref[cols, :] = x_ref[:, cols].T
        dyt_ref[cols, :] = dy_ref[:, cols].T


def vmem_call(body, out_shapes, inputs, scratch=(), smem=0, flops=0):
    inside = pl.BlockSpec(memory_space=pltpu.VMEM)
    scalar = pl.BlockSpec(memory_space=pltpu.SMEM)
    moved = sum(a.size * a.dtype.itemsize for a in (*inputs, *out_shapes))
    return pl.pallas_call(
        body,
        out_shape=out_shapes,
        in_specs=[scalar] * smem + [inside] * (len(inputs) - smem),
        out_specs=[inside] * len(out_shapes),
        scratch_shapes=list(scratch),
        compiler_params=pltpu.CompilerParams(vmem_limit_bytes=VMEM_LIMIT),
        cost_estimate=pl.CostEstimate(flops=flops, bytes_accessed=moved, transcendentals=0),
    )(*inputs)


def shape(*dims):
    return jax.ShapeDtypeStruct(dims, jnp.bfloat16)


def pack(hits, weights, scales):
    rows, _, experts = weights[0].shape
    held = pltpu.VMEM((3 * rows * experts, LANES), jnp.float32)
    wide = pltpu.VMEM((rows, experts), jnp.float32)
    return vmem_call(
        pack_kernel, [shape(hits.shape[0], rows, 896)], (hits.reshape(-1), *weights, *scales), (held, wide), 1
    )[0]


def settle(hits, received, like):
    rows, _, experts = like.shape
    acc = pltpu.VMEM((3, experts * rows, LANES), jnp.float32)
    return vmem_call(settle_kernel, [shape(*like.shape)] * 3, (hits.reshape(-1), received), (acc,), 1)


def per_device(
    tokens,
    route_slot,
    route_code,
    group_hits,
    gate_w,
    up_w,
    down_w,
    gate_scale,
    up_scale,
    down_scale,
    cotangent,
):
    hit_count = group_hits.shape[1]
    groups = group_hits.shape[0]
    owner_rows = gate_w.shape[0]
    codes = route_code.astype(jnp.float32)
    shares = codes / jnp.sum(codes, axis=1, keepdims=True)
    slots = jnp.arange(hit_count, dtype=jnp.int32)
    picked = (route_slot[:, :, None] == slots[None, None, :]).astype(jnp.float32)
    rweight = jnp.sum(picked * shares[:, :, None], axis=1).astype(jnp.bfloat16)
    sent = pack(group_hits, (gate_w, up_w, down_w), (gate_scale, up_scale, down_scale))
    received = lax.all_to_all(sent, "wide", split_axis=0, concat_axis=0, tiled=True)
    group_x = lax.all_gather(tokens, "narrow", axis=0, tiled=True)
    group_dy = lax.all_gather(cotangent, "narrow", axis=0, tiled=True)
    group_rw = lax.all_gather(rweight, "narrow", axis=0, tiled=True)
    tok, width = group_x.shape
    flipped = vmem_call(flip_kernel, [shape(width, tok)] * 2, (group_x, group_dy))
    weights = received.reshape(width, 896)
    terms, act = vmem_call(
        middle_kernel,
        [shape(width, 896), shape(tok, 1024)],
        (group_x, group_dy, *flipped, group_rw, weights),
        flops=2 * 6 * tok * width * 288,
    )
    back = lax.all_to_all(
        terms.reshape(groups, owner_rows, 896), "wide", split_axis=0, concat_axis=0, tiled=True
    )
    mixed, token_grad = vmem_call(
        out_kernel, [shape(tok, width)] * 2, (act, weights), flops=2 * 3 * tok * width * 288
    )
    mixed = lax.psum_scatter(mixed, "narrow", scatter_dimension=0, tiled=True)
    token_grad = lax.psum_scatter(token_grad, "narrow", scatter_dimension=0, tiled=True)
    gate_grad, up_grad, down_grad = settle(group_hits, back, gate_w)
    return (mixed, token_grad, gate_grad, up_grad, down_grad)


def solution(mesh):
    placed = (
        P(("wide", "narrow"), None),
        P(("wide", "narrow"), None),
        P(("wide", "narrow"), None),
        P(),
        P("wide", "narrow", None),
        P("wide", "narrow", None),
        P("wide", "narrow", None),
        P("wide", None),
        P("wide", None),
        P("wide", None),
        P(("wide", "narrow"), None),
    )
    return jax.shard_map(
        per_device,
        mesh=mesh,
        in_specs=placed,
        out_specs=(
            P(("wide", "narrow"), None),
            P(("wide", "narrow"), None),
            P("wide", "narrow", None),
            P("wide", "narrow", None),
            P("wide", "narrow", None),
        ),
        check_vma=False,
    )
```

```python
import jax
import jax.numpy as jnp
from jax import lax
from jax.experimental import pallas as pl
from jax.experimental.pallas import tpu as pltpu
from jax.sharding import PartitionSpec as P

LANES = 128
MIB = 1024 * 1024
PARTS = 8

COLUMNS = 896


def lane_index(shape):
    return lax.broadcasted_iota(jnp.int32, shape, len(shape) - 1)


def batched(count, size, load, store):
    @pl.loop(0, count // size)
    def _(i):
        values = [load(i * size + j) for j in range(size)]
        for j in range(size):
            store(i * size + j, values[j])


def pack_kernel(hits_ref, gate_ref, up_ref, down_ref, gs_ref, us_ref, ds_ref, out_ref, held, wide, ready, sem):
    rows, block, experts = gate_ref.shape
    groups = out_ref.shape[0]
    for m, s_ref in enumerate((gs_ref, us_ref, ds_ref)):
        wide[m] = s_ref[...].astype(jnp.float32)

    def scaled(r):
        flipped = []
        for m, w_ref in enumerate((gate_ref, up_ref, down_ref)):
            w = (w_ref[r].astype(jnp.float32) * wide[m, pl.ds(r, 1), :]).astype(jnp.bfloat16)
            w = jnp.concatenate([w, jnp.zeros((LANES - block, experts), jnp.bfloat16)], axis=0)
            flipped.append(w.astype(jnp.float32).T)
        return flipped

    def keep(r, flipped):
        for m in range(3):
            held[m, pl.ds(r, experts, stride=rows), :] = flipped[m]

    batched(rows, 4, scaled, keep)
    lane = lane_index((rows, LANES))

    def message(g):
        tiles, tail = [], jnp.zeros((rows, LANES), jnp.bfloat16)
        starts = [pl.multiple_of(hits_ref[k, g] * rows, rows) for k in range(3)]
        for m in range(3):
            first, second, third = [held[m, pl.ds(s, rows), :].astype(jnp.bfloat16) for s in starts]
            moved = pltpu.roll(second, 96, 1)
            last = pltpu.roll(third, 64, 1)
            tiles.append(jnp.where(lane < 96, first, moved))
            tiles.append(jnp.where(lane < 64, moved, last))
            rest = last if m == 0 else third if m == 2 else pltpu.roll(third, 96, 1)
            tail = jnp.where((lane >= 32 * m) & (lane < 32 * m + 32), rest, tail)
        return tiles + [tail]

    def emit(g, tiles):
        for q, tile in enumerate(tiles):
            ready[g, :, LANES * q : LANES * q + LANES] = tile

    size = groups // PARTS

    def move(i):
        part = pl.ds(i * size, size)
        return pltpu.make_async_copy(ready.at[part], out_ref.at[part], sem.at[i])

    for i in range(PARTS):
        batched(size, 4, lambda g, i=i: message(i * size + g), lambda g, t, i=i: emit(i * size + g, t))
        move(i).start()
    for i in range(PARTS):
        move(i).wait()


def settle_kernel(places_ref, recv_ref, gate_ref, up_ref, down_ref, here, norm, acc, sem):
    rows, block, experts = gate_ref.shape
    groups = recv_ref.shape[0]
    size = groups // PARTS

    def move(i):
        part = pl.ds(i * size, size)
        return pltpu.make_async_copy(recv_ref.at[part], here.at[part], sem.at[i])

    for i in range(PARTS):
        move(i).start()
    lane = lane_index((rows, LANES))

    def terms(g):
        tail = here[g, :, 768:896]
        out = []
        for m in range(3):
            low = here[g, :, 256 * m : 256 * m + 128]
            high = here[g, :, 256 * m + 128 : 256 * m + 256]
            second = pltpu.roll(jnp.where(lane < 64, high, low), 32, 1)
            if m == 0:
                third = pltpu.roll(jnp.where(lane < 64, tail, high), 64, 1)
            else:
                rest = tail if m == 2 else pltpu.roll(tail, 32, 1)
                third = jnp.where(lane < 64, pltpu.roll(high, 64, 1), rest)
            out.append((low, second, third))
        return out

    def keep(g, out):
        for m in range(3):
            for k in range(3):
                norm[m, 3 * g + k] = out[m][k]

    for i in range(PARTS):
        move(i).wait()
        batched(size, 4, lambda g, i=i: terms(i * size + g), lambda g, t, i=i: keep(i * size + g, t))

    def total(e):
        spots = [places_ref[q, e] for q in range(3)]
        out = []
        for m in range(3):
            a, b, c = [norm[m, s].astype(jnp.float32) for s in spots]
            out.append(a + b + c)
        return out

    def put(e, out):
        for m in range(3):
            acc[m, pl.ds(pl.multiple_of(e * rows, rows), rows), :] = out[m]

    batched(experts, 8, total, put)
    refs = (gate_ref, up_ref, down_ref)

    def flipped(r):
        return [acc[m, pl.ds(r, experts, stride=rows), :].T[:block].astype(jnp.bfloat16) for m in range(3)]

    def finish(r, out):
        for m in range(3):
            refs[m][r] = out[m]

    batched(rows, 4, flipped, finish)


def dot(left, right):
    return lax.dot_general(left, right, (((1,), (0,)), ((), ())), preferred_element_type=jnp.float32)


def dot_t(left, right):
    return lax.dot_general(left, right, (((1,), (1,)), ((), ())), preferred_element_type=jnp.float32)


def middle_kernel(x_ref, dy_ref, xt_ref, dyt_ref, rw_ref, w_ref, term_ref, act_ref, here, ready, in_sem, out_sem):
    tok, width = x_ref.shape
    spans = ((0, 256), (256, 256), (768, 128), (512, 256))

    def fetch(i):
        cols = pl.ds(*spans[i])
        return pltpu.make_async_copy(w_ref.at[:, cols], here.at[:, cols], in_sem.at[i])

    for i in range(4):
        fetch(i).start()
    rw = rw_ref[...].astype(jnp.float32)

    def finish(gate, up, back, share):
        sig = jax.nn.sigmoid(gate)
        silu = gate * sig
        weighted = share * silu * up
        d_act = share * back
        d_gate = d_act * up * sig * (1.0 + gate * (1.0 - sig))
        return d_gate, d_act * silu, weighted

    fetch(0).wait()
    gate = dot(x_ref[...], here[:, 0:256])
    fetch(1).wait()
    up = dot(x_ref[...], here[:, 256:512])
    fetch(2).wait()
    tail_x = dot(x_ref[...], here[:, 768:896])
    tail_dy = dot(dy_ref[...], here[:, 768:896])
    fetch(3).wait()
    back = dot(dy_ref[...], here[:, 512:768])
    lane = lane_index((tok, LANES))
    d_gate, d_up, weighted = finish(tail_x, pltpu.roll(tail_x, 96, 1), pltpu.roll(tail_dy, 64, 1), rw[:, 2:3])
    from_x = jnp.where(lane < 32, d_gate, jnp.where(lane < 64, pltpu.roll(d_up, 32, 1), 0.0))
    from_dy = jnp.where((lane >= 64) & (lane < 96), pltpu.roll(weighted, 64, 1), 0.0)
    act_ref[:, 768:896] = from_x.astype(jnp.bfloat16)
    act_ref[:, 896:1024] = from_dy.astype(jnp.bfloat16)
    lane = lane_index((tok, 256))
    share = jnp.where(lane < 96, rw[:, 0:1], jnp.where(lane < 192, rw[:, 1:2], rw[:, 2:3]))
    d_gate, d_up, weighted = finish(gate, up, back, share)
    act_ref[:, 0:256] = d_gate.astype(jnp.bfloat16)
    act_ref[:, 256:512] = d_up.astype(jnp.bfloat16)
    act_ref[:, 512:768] = weighted.astype(jnp.bfloat16)
    size = 512

    def send(i):
        part = pl.ds(pl.multiple_of(i * size, size), size)
        return pltpu.make_async_copy(ready.at[part], term_ref.at[part], out_sem.at[i])

    @pl.loop(0, width // size)
    def _(i):
        cols = pl.ds(pl.multiple_of(i * size, size), size)
        xt = xt_ref[cols, :]
        dyt = dyt_ref[cols, :]
        ready[cols, 0:256] = dot(xt, act_ref[:, 0:256]).astype(jnp.bfloat16)
        ready[cols, 256:512] = dot(xt, act_ref[:, 256:512]).astype(jnp.bfloat16)
        ready[cols, 512:768] = dot(dyt, act_ref[:, 512:768]).astype(jnp.bfloat16)
        tail = dot(xt, act_ref[:, 768:896]) + dot(dyt, act_ref[:, 896:1024])
        ready[cols, 768:896] = tail.astype(jnp.bfloat16)
        send(i).start()

    for i in range(width // size):
        send(i).wait()


def out_kernel(act_ref, w_ref, *outs):
    width = w_ref.shape[0]
    size = outs[0].shape[0]

    @pl.loop(0, width // 512)
    def _(i):
        start = pl.multiple_of(i * 512, 512)
        cols = pl.ds(start, 512)
        tail = w_ref[cols, 768:896]
        mixed = dot_t(act_ref[:, 512:768], w_ref[cols, 512:768]) + dot_t(act_ref[:, 896:1024], tail)
        grad = dot_t(act_ref[:, 0:512], w_ref[cols, 0:512]) + dot_t(act_ref[:, 768:896], tail)
        for s, out_ref in enumerate(outs):
            part = slice(s * size, s * size + size)
            out_ref[:, cols] = mixed[part].astype(jnp.bfloat16)
            out_ref[:, pl.ds(pl.multiple_of(start + width, 512), 512)] = grad[part].astype(jnp.bfloat16)


def flip_kernel(hits_ref, *refs):
    *blocks, places_ref, x_ref, dy_ref, xt_ref, dyt_ref, rw_ref, count = refs
    slots, groups = hits_ref.shape
    experts = places_ref.shape[1]
    size = blocks[0].shape[0]
    width = x_ref.shape[1]
    for s, ref in enumerate(blocks):
        rows = pl.ds(s * size, size)
        x_ref[rows, :] = ref[:, 0:width]
        dy_ref[rows, :] = ref[:, width : 2 * width]
        rw_ref[rows, :] = ref[:, 2 * width :]

    @pl.loop(0, width // 512)
    def _(i):
        cols = pl.ds(pl.multiple_of(i * 512, 512), 512)
        xt_ref[cols, :] = x_ref[:, cols].T
        dyt_ref[cols, :] = dy_ref[:, cols].T

    @pl.loop(0, experts)
    def _(e):
        count[e] = 0

    @pl.loop(0, groups)
    def _(g):
        for k in range(slots):
            e = hits_ref[k, g]
            seen = count[e]
            places_ref[seen, e] = slots * g + k
            count[e] = seen + 1


def call(body, outputs, inputs, spaces, out_spaces, scratch=(), limit=16, flops=0):
    moved = sum(a.size * a.dtype.itemsize for a in (*inputs, *outputs))
    return pl.pallas_call(
        body,
        out_shape=outputs,
        in_specs=[pl.BlockSpec(memory_space=s) for s in spaces],
        out_specs=[pl.BlockSpec(memory_space=s) for s in out_spaces],
        scratch_shapes=list(scratch),
        compiler_params=pltpu.CompilerParams(vmem_limit_bytes=limit * MIB),
        cost_estimate=pl.CostEstimate(flops=flops, bytes_accessed=moved, transcendentals=0),
    )(*inputs)


VMEM, SMEM, ANY = pltpu.VMEM, pltpu.SMEM, pl.ANY


def shape(*dims):
    return jax.ShapeDtypeStruct(dims, jnp.bfloat16)


def pack(hits, weights, scales):
    rows, _, experts = weights[0].shape
    groups = hits.shape[1]
    scratch = (
        VMEM((3, rows * experts, LANES), jnp.float32),
        VMEM((3, rows, experts), jnp.float32),
        VMEM((groups, rows, COLUMNS), jnp.bfloat16),
        pltpu.SemaphoreType.DMA((PARTS,)),
    )
    return call(
        pack_kernel,
        [shape(groups, rows, COLUMNS)],
        (hits, *weights, *scales),
        [SMEM] + [VMEM] * 6,
        [ANY],
        scratch,
        limit=60,
    )[0]


def settle(places, received, like):
    rows, _, experts = like.shape
    groups = received.shape[0]
    scratch = (
        VMEM((groups, rows, COLUMNS), jnp.bfloat16),
        VMEM((3, 3 * groups, rows, LANES), jnp.bfloat16),
        VMEM((3, experts * rows, LANES), jnp.float32),
        pltpu.SemaphoreType.DMA((PARTS,)),
    )
    return call(
        settle_kernel, [shape(*like.shape)] * 3, (places, received), [SMEM, ANY], [VMEM] * 3, scratch, limit=60
    )


def middle(x, dy, xt, dyt, rw, weights):
    tok, width = x.shape
    scratch = (
        VMEM((width, COLUMNS), jnp.bfloat16),
        VMEM((width, COLUMNS), jnp.bfloat16),
        pltpu.SemaphoreType.DMA((4,)),
        pltpu.SemaphoreType.DMA((width // 512,)),
    )
    return call(
        middle_kernel,
        [shape(width, COLUMNS), shape(tok, 1024)],
        (x, dy, xt, dyt, rw, weights),
        [VMEM] * 5 + [ANY],
        [ANY, VMEM],
        scratch,
        limit=32,
        flops=2 * 6 * tok * width * 288,
    )


def outputs(act, weights, devices):
    tok = act.shape[0]
    width = weights.shape[0]
    return call(
        out_kernel,
        [shape(tok // devices, 2 * width)] * devices,
        (act, weights),
        [VMEM] * 2,
        [VMEM] * devices,
        limit=60,
        flops=2 * 3 * tok * width * 288,
    )


def flip(hits, blocks, width, experts):
    tok = blocks[0].shape[0] * len(blocks)
    return call(
        flip_kernel,
        [jax.ShapeDtypeStruct((hits.shape[0], experts), jnp.int32)]
        + [shape(tok, width)] * 2
        + [shape(width, tok)] * 2
        + [shape(tok, LANES)],
        (hits, *blocks),
        [SMEM] + [VMEM] * len(blocks),
        [SMEM] + [VMEM] * 5,
        (SMEM((experts,), jnp.int32),),
        limit=60,
    )


def per_device(
    tokens,
    route_slot,
    route_code,
    group_hits,
    gate_w,
    up_w,
    down_w,
    gate_scale,
    up_scale,
    down_scale,
    cotangent,
):
    hit_count = group_hits.shape[1]
    groups = group_hits.shape[0]
    devices = lax.axis_size("narrow")
    owner_rows, _, experts = gate_w.shape
    width = tokens.shape[1]
    hits = group_hits.T
    codes = route_code.astype(jnp.float32)
    shares = codes / jnp.sum(codes, axis=1, keepdims=True)
    slots = jnp.arange(LANES, dtype=jnp.int32)
    picked = (route_slot[:, :, None] == slots[None, None, :]).astype(jnp.float32)
    rweight = jnp.sum(picked * shares[:, :, None], axis=1).astype(jnp.bfloat16)
    sent = pack(hits, (gate_w, up_w, down_w), (gate_scale, up_scale, down_scale))
    received = lax.all_to_all(sent, "wide", split_axis=0, concat_axis=0, tiled=True)
    weights = received.reshape(width, COLUMNS)

    def shift(value, step):
        return lax.ppermute(value, "narrow", [(i, (i + step) % devices) for i in range(devices)])

    mine = jnp.concatenate([tokens, cotangent, rweight], axis=1)
    blocks = [mine] + [shift(mine, s) for s in range(1, devices)]
    places, *gathered = flip(hits, blocks, width, experts)
    terms, act = middle(*gathered, weights)
    back = lax.all_to_all(
        terms.reshape(groups, owner_rows, COLUMNS), "wide", split_axis=0, concat_axis=0, tiled=True
    )
    parts = outputs(act, weights, devices)
    parts = [parts[0]] + [shift(parts[s], devices - s) for s in range(1, devices)]
    total = sum(p.astype(jnp.float32) for p in parts).astype(jnp.bfloat16)
    mixed, token_grad = total[:, :width], total[:, width:]
    gate_grad, up_grad, down_grad = settle(places, back, gate_w)
    return (mixed, token_grad, gate_grad, up_grad, down_grad)


def solution(mesh):
    placed = (
        P(("wide", "narrow"), None),
        P(("wide", "narrow"), None),
        P(("wide", "narrow"), None),
        P(),
        P("wide", "narrow", None),
        P("wide", "narrow", None),
        P("wide", "narrow", None),
        P("wide", None),
        P("wide", None),
        P("wide", None),
        P(("wide", "narrow"), None),
    )
    return jax.shard_map(
        per_device,
        mesh=mesh,
        in_specs=placed,
        out_specs=(
            P(("wide", "narrow"), None),
            P(("wide", "narrow"), None),
            P("wide", "narrow", None),
            P("wide", "narrow", None),
            P("wide", "narrow", None),
        ),
        check_vma=False,
    )
```

```python
import jax
import jax.numpy as jnp
from jax import lax
from jax.experimental import pallas as pl
from jax.experimental.pallas import tpu as pltpu
from jax.sharding import PartitionSpec as P

LANES = 128
MIB = 1024 * 1024
PARTS = 8
STEPS = 4
AHEAD = 4
SIZE = 512
CHUNK = 256

COLUMNS = 896


def lane_index(shape):
    return lax.broadcasted_iota(jnp.int32, shape, len(shape) - 1)


def batched(count, size, load, store):
    @pl.loop(0, count // size)
    def _(i):
        values = [load(i * size + j) for j in range(size)]
        for j in range(size):
            store(i * size + j, values[j])


def pack_kernel(
    hits_ref, gate_hbm, up_hbm, down_hbm, gs_ref, us_ref, ds_ref, out_ref, stored, held, wide, ready, in_sem, sem
):
    _, rows, block, experts = stored.shape
    groups = out_ref.shape[0]
    fetches = [
        pltpu.make_async_copy(w_hbm, stored.at[m], in_sem.at[m])
        for m, w_hbm in enumerate((gate_hbm, up_hbm, down_hbm))
    ]
    for copy in fetches:
        copy.start()
    for m, s_ref in enumerate((gs_ref, us_ref, ds_ref)):
        wide[m] = s_ref[...].astype(jnp.float32)
    for m in range(3):
        fetches[m].wait()

        def scaled(r, m=m):
            w = (stored[m, r].astype(jnp.float32) * wide[m, pl.ds(r, 1), :]).astype(jnp.bfloat16)
            w = jnp.concatenate([w, jnp.zeros((LANES - block, experts), jnp.bfloat16)], axis=0)
            return w.T.astype(jnp.float32)

        def keep(r, flipped, m=m):
            held[m, pl.ds(r, experts, stride=rows), :] = flipped

        batched(rows, 16, scaled, keep)
    lane = lane_index((rows, LANES))

    def message(g):
        tiles, tail = [], jnp.zeros((rows, LANES), jnp.bfloat16)
        starts = [pl.multiple_of(hits_ref[k, g] * rows, rows) for k in range(3)]
        for m in range(3):
            first, second, third = [held[m, pl.ds(s, rows), :].astype(jnp.bfloat16) for s in starts]
            moved = pltpu.roll(second, 96, 1)
            last = pltpu.roll(third, 64, 1)
            tiles.append(jnp.where(lane < 96, first, moved))
            tiles.append(jnp.where(lane < 64, moved, last))
            rest = last if m == 0 else third if m == 2 else pltpu.roll(third, 96, 1)
            tail = jnp.where((lane >= 32 * m) & (lane < 32 * m + 32), rest, tail)
        return tiles + [tail]

    def emit(g, tiles):
        for q, tile in enumerate(tiles):
            ready[g, :, LANES * q : LANES * q + LANES] = tile

    size = groups // PARTS

    def move(i):
        part = pl.ds(i * size, size)
        return pltpu.make_async_copy(ready.at[part], out_ref.at[part], sem.at[i])

    for i in range(PARTS):
        batched(size, 16, lambda g, i=i: message(i * size + g), lambda g, t, i=i: emit(i * size + g, t))
        move(i).start()
    for i in range(PARTS):
        move(i).wait()


def settle_kernel(places_ref, recv_ref, gate_ref, up_ref, down_ref, here, norm, acc, sem):
    rows, block, experts = gate_ref.shape
    groups = recv_ref.shape[0]
    size = groups // PARTS

    def move(i):
        part = pl.ds(i * size, size)
        return pltpu.make_async_copy(recv_ref.at[part], here.at[part], sem.at[i])

    for i in range(PARTS):
        move(i).start()
    lane = lane_index((rows, LANES))

    def terms(g):
        tail = here[g, :, 768:896]
        out = []
        for m in range(3):
            low = here[g, :, 256 * m : 256 * m + 128]
            high = here[g, :, 256 * m + 128 : 256 * m + 256]
            second = pltpu.roll(jnp.where(lane < 64, high, low), 32, 1)
            if m == 0:
                third = pltpu.roll(jnp.where(lane < 64, tail, high), 64, 1)
            else:
                rest = tail if m == 2 else pltpu.roll(tail, 32, 1)
                third = jnp.where(lane < 64, pltpu.roll(high, 64, 1), rest)
            out.append((low, second, third))
        return out

    def keep(g, out):
        for m in range(3):
            for k in range(3):
                norm[m, 3 * g + k] = out[m][k]

    for i in range(PARTS):
        move(i).wait()
        batched(size, 16, lambda g, i=i: terms(i * size + g), lambda g, t, i=i: keep(i * size + g, t))

    def total(e):
        spots = [places_ref[q, e] for q in range(3)]
        out = []
        for m in range(3):
            a, b, c = [norm[m, s].astype(jnp.float32) for s in spots]
            out.append(a + b + c)
        return out

    def put(e, out):
        for m in range(3):
            acc[m, pl.ds(pl.multiple_of(e * rows, rows), rows), :] = out[m]

    batched(experts, 16, total, put)
    refs = (gate_ref, up_ref, down_ref)

    def flipped(r):
        return [acc[m, pl.ds(r, experts, stride=rows), :].astype(jnp.bfloat16).T[:block] for m in range(3)]

    def finish(r, out):
        for m in range(3):
            refs[m][r] = out[m]

    batched(rows, 8, flipped, finish)


def dot(left, right):
    return lax.dot_general(left, right, (((1,), (0,)), ((), ())), preferred_element_type=jnp.float32)


def dot_t(left, right):
    return lax.dot_general(left, right, (((1,), (1,)), ((), ())), preferred_element_type=jnp.float32)


def middle_kernel(
    x_hbm, dy_hbm, xt_hbm, dyt_hbm, rw_hbm, w_hbm, term_ref, act_ref, x, dy, xt, dyt, rw, w, act, ready, pre, sem, flip_sem, out_sem
):
    tok, width = x.shape

    steps = STEPS
    depth = width // steps

    def arriving(i):
        part = pl.ds(i * depth, depth)
        pairs = ((x_hbm.at[:, part], x.at[:, part]), (dy_hbm.at[:, part], dy.at[:, part]), (w_hbm.at[part], w.at[part]))
        return [pltpu.make_async_copy(*pair, sem.at[3 * i + j]) for j, pair in enumerate(pairs)]

    def flipped(i):
        part = pl.ds(i * size, size)
        pairs = ((xt_hbm.at[part], xt.at[part]), (dyt_hbm.at[part], dyt.at[part]))
        return [pltpu.make_async_copy(*pair, flip_sem.at[2 * i + j]) for j, pair in enumerate(pairs)]

    size = SIZE
    waiting = [arriving(i) for i in range(steps)]
    waiting.append([pltpu.make_async_copy(rw_hbm, rw, sem.at[3 * steps])])
    waiting += [flipped(i) for i in range(width // size)]
    for group in waiting[:AHEAD]:
        for copy in group:
            copy.start()
    started = AHEAD
    for i in range(steps):
        for copy in waiting[i]:
            copy.wait()
        for copy in waiting[started] if started < len(waiting) else ():
            copy.start()
        started += 1
        part = pl.ds(i * depth, depth)
        for left, cols in ((x, slice(0, 512)), (x, slice(768, 896)), (dy, slice(512, 768)), (dy, slice(768, 896))):
            to = slice(896, 1024) if left is dy and cols.start == 768 else cols
            term = dot(left[:, part], w[part, cols])
            pre[:, to] = term if i == 0 else pre[:, to] + term
    for group in waiting[started:]:
        for copy in group:
            copy.start()
    waiting[steps][0].wait()

    def finish(gate, up, back, share):
        sig = jax.nn.sigmoid(gate)
        silu = gate * sig
        weighted = share * silu * up
        d_act = share * back
        d_gate = d_act * up * sig * (1.0 + gate * (1.0 - sig))
        return d_gate, d_act * silu, weighted

    chunk = CHUNK
    lane = lane_index((chunk, LANES))

    @pl.loop(0, tok // chunk)
    def _(i):
        rows = pl.ds(pl.multiple_of(i * chunk, chunk), chunk)
        share = rw[rows, :].astype(jnp.float32)
        one, two, three = share[:, 0:1], share[:, 1:2], share[:, 2:3]
        for h, part in enumerate((jnp.where(lane < 96, one, two), jnp.where(lane < 64, two, three))):
            at = [slice(256 * m + 128 * h, 256 * m + 128 * h + 128) for m in range(3)]
            for span, value in zip(at, finish(*[pre[rows, span] for span in at], part)):
                act[rows, span] = value.astype(jnp.bfloat16)
        tail_x, tail_dy = pre[rows, 768:896], pre[rows, 896:1024]
        d_gate, d_up, weighted = finish(tail_x, pltpu.roll(tail_x, 96, 1), pltpu.roll(tail_dy, 64, 1), three)
        from_x = jnp.where(lane < 32, d_gate, jnp.where(lane < 64, pltpu.roll(d_up, 32, 1), 0.0))
        from_dy = jnp.where((lane >= 64) & (lane < 96), pltpu.roll(weighted, 64, 1), 0.0)
        act[rows, 768:896] = from_x.astype(jnp.bfloat16)
        act[rows, 896:1024] = from_dy.astype(jnp.bfloat16)

    put_act = pltpu.make_async_copy(act, act_ref, sem.at[3 * steps + 1])
    put_act.start()

    def send(i):
        part = pl.ds(pl.multiple_of(i * size, size), size)
        return pltpu.make_async_copy(ready.at[part], term_ref.at[part], out_sem.at[i])

    for group in waiting[steps + 1 :]:
        for copy in group:
            copy.wait()
    for i in range(width // size):
        cols = pl.ds(i * size, size)
        left, right = xt[cols, :], dyt[cols, :]
        ready[cols, 0:512] = dot(left, act[:, 0:512]).astype(jnp.bfloat16)
        ready[cols, 512:768] = dot(right, act[:, 512:768]).astype(jnp.bfloat16)
        tail = dot(left, act[:, 768:896]) + dot(right, act[:, 896:1024])
        ready[cols, 768:896] = tail.astype(jnp.bfloat16)
        send(i).start()

    put_act.wait()
    for i in range(width // size):
        send(i).wait()


def out_kernel(act_ref, w_ref, *outs):
    width = w_ref.shape[0]
    size = outs[0].shape[0]

    @pl.loop(0, width // 512)
    def _(i):
        start = pl.multiple_of(i * 512, 512)
        cols = pl.ds(start, 512)
        tail = w_ref[cols, 768:896]
        mixed = dot_t(act_ref[:, 512:768], w_ref[cols, 512:768]) + dot_t(act_ref[:, 896:1024], tail)
        grad = dot_t(act_ref[:, 0:512], w_ref[cols, 0:512]) + dot_t(act_ref[:, 768:896], tail)
        for s, out_ref in enumerate(outs):
            part = slice(s * size, s * size + size)
            out_ref[:, cols] = mixed[part].astype(jnp.bfloat16)
            out_ref[:, pl.ds(pl.multiple_of(start + width, 512), 512)] = grad[part].astype(jnp.bfloat16)


def flip_kernel(hits_ref, *refs):
    *blocks, places_ref, x_ref, dy_ref, xt_ref, dyt_ref, rw_ref, count = refs
    slots, groups = hits_ref.shape
    experts = places_ref.shape[1]
    size = blocks[0].shape[0]
    width = x_ref.shape[1]
    for s, ref in enumerate(blocks):
        rows = pl.ds(s * size, size)
        x_ref[rows, :] = ref[:, 0:width]
        dy_ref[rows, :] = ref[:, width : 2 * width]
        rw_ref[rows, :] = ref[:, 2 * width :]

    @pl.loop(0, width // 512)
    def _(i):
        cols = pl.ds(pl.multiple_of(i * 512, 512), 512)
        xt_ref[cols, :] = x_ref[:, cols].T
        dyt_ref[cols, :] = dy_ref[:, cols].T

    @pl.loop(0, experts)
    def _(e):
        count[e] = 0

    @pl.loop(0, groups)
    def _(g):
        for k in range(slots):
            e = hits_ref[k, g]
            seen = count[e]
            places_ref[seen, e] = slots * g + k
            count[e] = seen + 1


def call(body, outputs, inputs, spaces, out_spaces, scratch=(), limit=16, flops=0):
    moved = sum(a.size * a.dtype.itemsize for a in (*inputs, *outputs))
    return pl.pallas_call(
        body,
        out_shape=outputs,
        in_specs=[pl.BlockSpec(memory_space=s) for s in spaces],
        out_specs=[pl.BlockSpec(memory_space=s) for s in out_spaces],
        scratch_shapes=list(scratch),
        compiler_params=pltpu.CompilerParams(vmem_limit_bytes=limit * MIB),
        cost_estimate=pl.CostEstimate(flops=flops, bytes_accessed=moved, transcendentals=0),
    )(*inputs)


VMEM, SMEM, ANY = pltpu.VMEM, pltpu.SMEM, pl.ANY


def shape(*dims):
    return jax.ShapeDtypeStruct(dims, jnp.bfloat16)


def pack(hits, weights, scales):
    rows, _, experts = weights[0].shape
    groups = hits.shape[1]
    scratch = (
        VMEM((3, *weights[0].shape), jnp.bfloat16),
        VMEM((3, rows * experts, LANES), jnp.float32),
        VMEM((3, rows, experts), jnp.float32),
        VMEM((groups, rows, COLUMNS), jnp.bfloat16),
        pltpu.SemaphoreType.DMA((3,)),
        pltpu.SemaphoreType.DMA((PARTS,)),
    )
    return call(
        pack_kernel,
        [shape(groups, rows, COLUMNS)],
        (hits, *weights, *scales),
        [SMEM] + [ANY] * 3 + [VMEM] * 3,
        [ANY],
        scratch,
        limit=60,
    )[0]


def settle(places, received, like):
    rows, _, experts = like.shape
    groups = received.shape[0]
    scratch = (
        VMEM((groups, rows, COLUMNS), jnp.bfloat16),
        VMEM((3, 3 * groups, rows, LANES), jnp.bfloat16),
        VMEM((3, experts * rows, LANES), jnp.float32),
        pltpu.SemaphoreType.DMA((PARTS,)),
    )
    return call(
        settle_kernel, [shape(*like.shape)] * 3, (places, received), [SMEM, ANY], [VMEM] * 3, scratch, limit=60
    )


def middle(x, dy, xt, dyt, rw, weights):
    tok, width = x.shape
    scratch = (
        *[VMEM(a.shape, jnp.bfloat16) for a in (x, dy, xt, dyt, rw, weights)],
        VMEM((tok, 1024), jnp.bfloat16),
        VMEM((width, COLUMNS), jnp.bfloat16),
        VMEM((tok, 1024), jnp.float32),
        pltpu.SemaphoreType.DMA((3 * STEPS + 2,)),
        pltpu.SemaphoreType.DMA((2 * width // SIZE,)),
        pltpu.SemaphoreType.DMA((width // SIZE,)),
    )
    return call(
        middle_kernel,
        [shape(width, COLUMNS), shape(tok, 1024)],
        (x, dy, xt, dyt, rw, weights),
        [ANY] * 6,
        [ANY, ANY],
        scratch,
        limit=60,
        flops=2 * 6 * tok * width * 288,
    )


def outputs(act, weights, devices):
    tok = act.shape[0]
    width = weights.shape[0]
    return call(
        out_kernel,
        [shape(tok // devices, 2 * width)] * devices,
        (act, weights),
        [VMEM] * 2,
        [VMEM] * devices,
        limit=60,
        flops=2 * 3 * tok * width * 288,
    )


def flip(hits, blocks, width, experts):
    tok = blocks[0].shape[0] * len(blocks)
    return call(
        flip_kernel,
        [jax.ShapeDtypeStruct((hits.shape[0], experts), jnp.int32)]
        + [shape(tok, width)] * 2
        + [shape(width, tok)] * 2
        + [shape(tok, LANES)],
        (hits, *blocks),
        [SMEM] + [VMEM] * len(blocks),
        [SMEM] + [VMEM] * 5,
        (SMEM((experts,), jnp.int32),),
        limit=60,
    )


def per_device(
    tokens,
    route_slot,
    route_code,
    group_hits,
    gate_w,
    up_w,
    down_w,
    gate_scale,
    up_scale,
    down_scale,
    cotangent,
):
    hit_count = group_hits.shape[1]
    groups = group_hits.shape[0]
    devices = lax.axis_size("narrow")
    owner_rows, _, experts = gate_w.shape
    width = tokens.shape[1]
    hits = group_hits.T
    codes = route_code.astype(jnp.float32)
    shares = codes / jnp.sum(codes, axis=1, keepdims=True)
    slots = jnp.arange(LANES, dtype=jnp.int32)
    picked = (route_slot[:, :, None] == slots[None, None, :]).astype(jnp.float32)
    rweight = jnp.sum(picked * shares[:, :, None], axis=1).astype(jnp.bfloat16)
    sent = pack(hits, (gate_w, up_w, down_w), (gate_scale, up_scale, down_scale))
    received = lax.all_to_all(sent, "wide", split_axis=0, concat_axis=0, tiled=True)
    weights = received.reshape(width, COLUMNS)

    def shift(value, step):
        return lax.ppermute(value, "narrow", [(i, (i + step) % devices) for i in range(devices)])

    mine = jnp.concatenate([tokens, cotangent, rweight], axis=1)
    blocks = [mine] + [shift(mine, s) for s in range(1, devices)]
    places, *gathered = flip(hits, blocks, width, experts)
    terms, act = middle(*gathered, weights)
    back = lax.all_to_all(
        terms.reshape(groups, owner_rows, COLUMNS), "wide", split_axis=0, concat_axis=0, tiled=True
    )
    parts = outputs(act, weights, devices)
    parts = [parts[0]] + [shift(parts[s], devices - s) for s in range(1, devices)]
    total = sum(p.astype(jnp.float32) for p in parts).astype(jnp.bfloat16)
    mixed, token_grad = total[:, :width], total[:, width:]
    gate_grad, up_grad, down_grad = settle(places, back, gate_w)
    return (mixed, token_grad, gate_grad, up_grad, down_grad)


def solution(mesh):
    placed = (
        P(("wide", "narrow"), None),
        P(("wide", "narrow"), None),
        P(("wide", "narrow"), None),
        P(),
        P("wide", "narrow", None),
        P("wide", "narrow", None),
        P("wide", "narrow", None),
        P("wide", None),
        P("wide", None),
        P("wide", None),
        P(("wide", "narrow"), None),
    )
    return jax.shard_map(
        per_device,
        mesh=mesh,
        in_specs=placed,
        out_specs=(
            P(("wide", "narrow"), None),
            P(("wide", "narrow"), None),
            P("wide", "narrow", None),
            P("wide", "narrow", None),
            P("wide", "narrow", None),
        ),
        check_vma=False,
    )
```

```python
import jax
import jax.numpy as jnp
from jax import lax
from jax.experimental import pallas as pl
from jax.experimental.pallas import tpu as pltpu
from jax.sharding import PartitionSpec as P

LANES = 128
MIB = 1024 * 1024
PARTS = 8
STEPS = 4
AHEAD = 4
SIZE = 512
CHUNK = 256

COLUMNS = 896


def lane_index(shape):
    return lax.broadcasted_iota(jnp.int32, shape, len(shape) - 1)


def batched(count, size, load, store):
    @pl.loop(0, count // size)
    def _(i):
        values = [load(i * size + j) for j in range(size)]
        for j in range(size):
            store(i * size + j, values[j])


def pack_kernel(
    hits_hbm,
    gate_hbm,
    up_hbm,
    down_hbm,
    gs_hbm,
    us_hbm,
    ds_hbm,
    out_ref,
    hits_ref,
    stored,
    scales,
    held,
    wide,
    ready,
    in_sem,
    sem,
):
    _, rows, block, experts = stored.shape
    groups = out_ref.shape[0]
    pairs = [(hits_hbm, hits_ref)]
    for m, (w_hbm, s_hbm) in enumerate(((gate_hbm, gs_hbm), (up_hbm, us_hbm), (down_hbm, ds_hbm))):
        pairs += [(s_hbm, scales.at[m]), (w_hbm, stored.at[m])]
    fetches = [pltpu.make_async_copy(*pair, in_sem.at[i]) for i, pair in enumerate(pairs)]
    for copy in fetches:
        copy.start()
    fetches[0].wait()
    for m in range(3):
        fetches[2 * m + 1].wait()
        fetches[2 * m + 2].wait()
        wide[m] = scales[m].astype(jnp.float32)

        def scaled(r, m=m):
            w = (stored[m, r].astype(jnp.float32) * wide[m, pl.ds(r, 1), :]).astype(jnp.bfloat16)
            w = jnp.concatenate([w, jnp.zeros((LANES - block, experts), jnp.bfloat16)], axis=0)
            return w.T.astype(jnp.float32)

        def keep(r, flipped, m=m):
            held[m, pl.ds(r, experts, stride=rows), :] = flipped

        batched(rows, 16, scaled, keep)
    lane = lane_index((rows, LANES))

    def message(g):
        tiles, tail = [], jnp.zeros((rows, LANES), jnp.bfloat16)
        starts = [pl.multiple_of(hits_ref[k, g] * rows, rows) for k in range(3)]
        for m in range(3):
            first, second, third = [held[m, pl.ds(s, rows), :].astype(jnp.bfloat16) for s in starts]
            moved = pltpu.roll(second, 96, 1)
            last = pltpu.roll(third, 64, 1)
            tiles.append(jnp.where(lane < 96, first, moved))
            tiles.append(jnp.where(lane < 64, moved, last))
            rest = last if m == 0 else third if m == 2 else pltpu.roll(third, 96, 1)
            tail = jnp.where((lane >= 32 * m) & (lane < 32 * m + 32), rest, tail)
        return tiles + [tail]

    def emit(g, tiles):
        for q, tile in enumerate(tiles):
            ready[g, :, LANES * q : LANES * q + LANES] = tile

    size = groups // PARTS

    def move(i):
        part = pl.ds(i * size, size)
        return pltpu.make_async_copy(ready.at[part], out_ref.at[part], sem.at[i])

    for i in range(PARTS):
        batched(size, 16, lambda g, i=i: message(i * size + g), lambda g, t, i=i: emit(i * size + g, t))
        move(i).start()
    for i in range(PARTS):
        move(i).wait()


def settle_kernel(
    places_hbm, recv_ref, gate_ref, up_ref, down_ref, places_ref, here, norm, acc, grads, sem, places_sem, out_sem
):
    _, rows, block, experts = grads.shape
    groups = recv_ref.shape[0]
    size = groups // PARTS

    def move(i):
        part = pl.ds(i * size, size)
        return pltpu.make_async_copy(recv_ref.at[part], here.at[part], sem.at[i])

    for i in range(PARTS):
        move(i).start()
    get_places = pltpu.make_async_copy(places_hbm, places_ref, places_sem)
    get_places.start()
    lane = lane_index((rows, LANES))

    def terms(g):
        tail = here[g, :, 768:896]
        out = []
        for m in range(3):
            low = here[g, :, 256 * m : 256 * m + 128]
            high = here[g, :, 256 * m + 128 : 256 * m + 256]
            second = pltpu.roll(jnp.where(lane < 64, high, low), 32, 1)
            if m == 0:
                third = pltpu.roll(jnp.where(lane < 64, tail, high), 64, 1)
            else:
                rest = tail if m == 2 else pltpu.roll(tail, 32, 1)
                third = jnp.where(lane < 64, pltpu.roll(high, 64, 1), rest)
            out.append((low, second, third))
        return out

    def keep(g, out):
        for m in range(3):
            for k in range(3):
                norm[m, 3 * g + k] = out[m][k]

    for i in range(PARTS):
        move(i).wait()
        batched(size, 16, lambda g, i=i: terms(i * size + g), lambda g, t, i=i: keep(i * size + g, t))

    def total(e):
        spots = [places_ref[q, e] for q in range(3)]
        out = []
        for m in range(3):
            a, b, c = [norm[m, s].astype(jnp.float32) for s in spots]
            out.append(a + b + c)
        return out

    def put(e, out):
        for m in range(3):
            acc[m, pl.ds(pl.multiple_of(e * rows, rows), rows), :] = out[m]

    get_places.wait()
    batched(experts, 16, total, put)

    def flipped(r):
        return [acc[m, pl.ds(r, experts, stride=rows), :].astype(jnp.bfloat16).T[:block] for m in range(3)]

    def finish(r, out):
        for m in range(3):
            grads[m, r] = out[m]

    puts = []
    for half in range(2):
        part = pl.ds(half * rows // 2, rows // 2)
        batched(rows // 2, 8, lambda r, h=half: flipped(h * rows // 2 + r), lambda r, out, h=half: finish(h * rows // 2 + r, out))
        for m, ref in enumerate((gate_ref, up_ref, down_ref)):
            puts.append(pltpu.make_async_copy(grads.at[m, part], ref.at[part], out_sem.at[3 * half + m]))
            puts[-1].start()
    for copy in puts:
        copy.wait()


def dot(left, right):
    return lax.dot_general(left, right, (((1,), (0,)), ((), ())), preferred_element_type=jnp.float32)


def dot_t(left, right):
    return lax.dot_general(left, right, (((1,), (1,)), ((), ())), preferred_element_type=jnp.float32)


def middle_kernel(
    x_hbm, dy_hbm, xt_hbm, dyt_hbm, rw_hbm, w_hbm, term_ref, act_ref, x, dy, xt, dyt, rw, w, act, ready, pre, sem, flip_sem, out_sem
):
    tok, width = x.shape

    steps = STEPS
    depth = width // steps

    def arriving(i):
        part = pl.ds(i * depth, depth)
        pairs = ((x_hbm.at[:, part], x.at[:, part]), (dy_hbm.at[:, part], dy.at[:, part]), (w_hbm.at[part], w.at[part]))
        return [pltpu.make_async_copy(*pair, sem.at[3 * i + j]) for j, pair in enumerate(pairs)]

    def flipped(i):
        part = pl.ds(i * size, size)
        pairs = ((xt_hbm.at[part], xt.at[part]), (dyt_hbm.at[part], dyt.at[part]))
        return [pltpu.make_async_copy(*pair, flip_sem.at[2 * i + j]) for j, pair in enumerate(pairs)]

    size = SIZE
    waiting = [arriving(i) for i in range(steps)]
    waiting.append([pltpu.make_async_copy(rw_hbm, rw, sem.at[3 * steps])])
    waiting += [flipped(i) for i in range(width // size)]
    for group in waiting[:AHEAD]:
        for copy in group:
            copy.start()
    started = AHEAD
    for i in range(steps):
        for copy in waiting[i]:
            copy.wait()
        for copy in waiting[started] if started < len(waiting) else ():
            copy.start()
        started += 1
        part = pl.ds(i * depth, depth)
        for left, cols in ((x, slice(0, 512)), (x, slice(768, 896)), (dy, slice(512, 768)), (dy, slice(768, 896))):
            to = slice(896, 1024) if left is dy and cols.start == 768 else cols
            term = dot(left[:, part], w[part, cols])
            pre[:, to] = term if i == 0 else pre[:, to] + term
    for group in waiting[started:]:
        for copy in group:
            copy.start()
    waiting[steps][0].wait()

    def finish(gate, up, back, share):
        sig = jax.nn.sigmoid(gate)
        silu = gate * sig
        weighted = share * silu * up
        d_act = share * back
        d_gate = d_act * up * sig * (1.0 + gate * (1.0 - sig))
        return d_gate, d_act * silu, weighted

    chunk = CHUNK
    lane = lane_index((chunk, LANES))

    for i in range(tok // chunk):
        rows = pl.ds(i * chunk, chunk)
        share = rw[rows, :].astype(jnp.float32)
        one, two, three = share[:, 0:1], share[:, 1:2], share[:, 2:3]
        for h, part in enumerate((jnp.where(lane < 96, one, two), jnp.where(lane < 64, two, three))):
            at = [slice(256 * m + 128 * h, 256 * m + 128 * h + 128) for m in range(3)]
            for span, value in zip(at, finish(*[pre[rows, span] for span in at], part)):
                act[rows, span] = value.astype(jnp.bfloat16)
        tail_x, tail_dy = pre[rows, 768:896], pre[rows, 896:1024]
        d_gate, d_up, weighted = finish(tail_x, pltpu.roll(tail_x, 96, 1), pltpu.roll(tail_dy, 64, 1), three)
        from_x = jnp.where(lane < 32, d_gate, jnp.where(lane < 64, pltpu.roll(d_up, 32, 1), 0.0))
        from_dy = jnp.where((lane >= 64) & (lane < 96), pltpu.roll(weighted, 64, 1), 0.0)
        act[rows, 768:896] = from_x.astype(jnp.bfloat16)
        act[rows, 896:1024] = from_dy.astype(jnp.bfloat16)

    put_act = pltpu.make_async_copy(act, act_ref, sem.at[3 * steps + 1])
    put_act.start()

    def send(i):
        part = pl.ds(pl.multiple_of(i * size, size), size)
        return pltpu.make_async_copy(ready.at[part], term_ref.at[part], out_sem.at[i])

    for group in waiting[steps + 1 :]:
        for copy in group:
            copy.wait()
    for i in range(width // size):
        cols = pl.ds(i * size, size)
        left, right = xt[cols, :], dyt[cols, :]
        ready[cols, 0:512] = dot(left, act[:, 0:512]).astype(jnp.bfloat16)
        ready[cols, 512:768] = dot(right, act[:, 512:768]).astype(jnp.bfloat16)
        tail = dot(left, act[:, 768:896]) + dot(right, act[:, 896:1024])
        ready[cols, 768:896] = tail.astype(jnp.bfloat16)
        send(i).start()

    put_act.wait()
    for i in range(width // size):
        send(i).wait()


def out_kernel(act_ref, w_ref, *outs):
    width = w_ref.shape[0]
    size = outs[0].shape[0]

    @pl.loop(0, width // 512)
    def _(i):
        start = pl.multiple_of(i * 512, 512)
        cols = pl.ds(start, 512)
        tail = w_ref[cols, 768:896]
        mixed = dot_t(act_ref[:, 512:768], w_ref[cols, 512:768]) + dot_t(act_ref[:, 896:1024], tail)
        grad = dot_t(act_ref[:, 0:512], w_ref[cols, 0:512]) + dot_t(act_ref[:, 768:896], tail)
        for s, out_ref in enumerate(outs):
            part = slice(s * size, s * size + size)
            out_ref[:, cols] = mixed[part].astype(jnp.bfloat16)
            out_ref[:, pl.ds(pl.multiple_of(start + width, 512), 512)] = grad[part].astype(jnp.bfloat16)


def flip_kernel(hits_ref, *refs):
    *blocks, places_ref, x_ref, dy_ref, xt_ref, dyt_ref, rw_ref, count = refs
    slots, groups = hits_ref.shape
    experts = places_ref.shape[1]
    size = blocks[0].shape[0]
    width = x_ref.shape[1]
    for s, ref in enumerate(blocks):
        rows = pl.ds(s * size, size)
        x_ref[rows, :] = ref[:, 0:width]
        dy_ref[rows, :] = ref[:, width : 2 * width]
        rw_ref[rows, :] = ref[:, 2 * width :]

    @pl.loop(0, width // 512)
    def _(i):
        cols = pl.ds(pl.multiple_of(i * 512, 512), 512)
        xt_ref[cols, :] = x_ref[:, cols].T
        dyt_ref[cols, :] = dy_ref[:, cols].T

    @pl.loop(0, experts)
    def _(e):
        count[e] = 0

    @pl.loop(0, groups)
    def _(g):
        for k in range(slots):
            e = hits_ref[k, g]
            seen = count[e]
            places_ref[seen, e] = slots * g + k
            count[e] = seen + 1


def call(body, outputs, inputs, spaces, out_spaces, scratch=(), limit=16, flops=0):
    moved = sum(a.size * a.dtype.itemsize for a in (*inputs, *outputs))
    return pl.pallas_call(
        body,
        out_shape=outputs,
        in_specs=[pl.BlockSpec(memory_space=s) for s in spaces],
        out_specs=[pl.BlockSpec(memory_space=s) for s in out_spaces],
        scratch_shapes=list(scratch),
        compiler_params=pltpu.CompilerParams(vmem_limit_bytes=limit * MIB),
        cost_estimate=pl.CostEstimate(flops=flops, bytes_accessed=moved, transcendentals=0),
    )(*inputs)


VMEM, SMEM, ANY = pltpu.VMEM, pltpu.SMEM, pl.ANY


def shape(*dims):
    return jax.ShapeDtypeStruct(dims, jnp.bfloat16)


def pack(hits, weights, scales):
    rows, _, experts = weights[0].shape
    groups = hits.shape[1]
    scratch = (
        SMEM(hits.shape, jnp.int32),
        VMEM((3, *weights[0].shape), jnp.bfloat16),
        VMEM((3, rows, experts), jnp.bfloat16),
        VMEM((3, rows * experts, LANES), jnp.float32),
        VMEM((3, rows, experts), jnp.float32),
        VMEM((groups, rows, COLUMNS), jnp.bfloat16),
        pltpu.SemaphoreType.DMA((7,)),
        pltpu.SemaphoreType.DMA((PARTS,)),
    )
    return call(
        pack_kernel,
        [shape(groups, rows, COLUMNS)],
        (hits, *weights, *scales),
        [ANY] * 7,
        [ANY],
        scratch,
        limit=60,
    )[0]


def settle(places, received, like):
    rows, _, experts = like.shape
    groups = received.shape[0]
    scratch = (
        SMEM(places.shape, jnp.int32),
        VMEM((groups, rows, COLUMNS), jnp.bfloat16),
        VMEM((3, 3 * groups, rows, LANES), jnp.bfloat16),
        VMEM((3, experts * rows, LANES), jnp.float32),
        VMEM((3, *like.shape), jnp.bfloat16),
        pltpu.SemaphoreType.DMA((PARTS,)),
        pltpu.SemaphoreType.DMA,
        pltpu.SemaphoreType.DMA((6,)),
    )
    return call(
        settle_kernel, [shape(*like.shape)] * 3, (places, received), [ANY] * 2, [ANY] * 3, scratch, limit=60
    )


def middle(x, dy, xt, dyt, rw, weights):
    tok, width = x.shape
    scratch = (
        *[VMEM(a.shape, jnp.bfloat16) for a in (x, dy, xt, dyt, rw, weights)],
        VMEM((tok, 1024), jnp.bfloat16),
        VMEM((width, COLUMNS), jnp.bfloat16),
        VMEM((tok, 1024), jnp.float32),
        pltpu.SemaphoreType.DMA((3 * STEPS + 2,)),
        pltpu.SemaphoreType.DMA((2 * width // SIZE,)),
        pltpu.SemaphoreType.DMA((width // SIZE,)),
    )
    return call(
        middle_kernel,
        [shape(width, COLUMNS), shape(tok, 1024)],
        (x, dy, xt, dyt, rw, weights),
        [ANY] * 6,
        [ANY, ANY],
        scratch,
        limit=60,
        flops=2 * 6 * tok * width * 288,
    )


def outputs(act, weights, devices):
    tok = act.shape[0]
    width = weights.shape[0]
    return call(
        out_kernel,
        [shape(tok // devices, 2 * width)] * devices,
        (act, weights),
        [VMEM] * 2,
        [VMEM] * devices,
        limit=60,
        flops=2 * 3 * tok * width * 288,
    )


def flip(hits, blocks, width, experts):
    tok = blocks[0].shape[0] * len(blocks)
    return call(
        flip_kernel,
        [jax.ShapeDtypeStruct((hits.shape[0], experts), jnp.int32)]
        + [shape(tok, width)] * 2
        + [shape(width, tok)] * 2
        + [shape(tok, LANES)],
        (hits, *blocks),
        [SMEM] + [VMEM] * len(blocks),
        [SMEM] + [VMEM] * 5,
        (SMEM((experts,), jnp.int32),),
        limit=60,
    )


def per_device(
    tokens,
    route_slot,
    route_code,
    group_hits,
    gate_w,
    up_w,
    down_w,
    gate_scale,
    up_scale,
    down_scale,
    cotangent,
):
    hit_count = group_hits.shape[1]
    groups = group_hits.shape[0]
    devices = lax.axis_size("narrow")
    owner_rows, _, experts = gate_w.shape
    width = tokens.shape[1]
    hits = group_hits.T
    codes = route_code.astype(jnp.float32)
    shares = codes / jnp.sum(codes, axis=1, keepdims=True)
    slots = jnp.arange(LANES, dtype=jnp.int32)
    picked = (route_slot[:, :, None] == slots[None, None, :]).astype(jnp.float32)
    rweight = jnp.sum(picked * shares[:, :, None], axis=1).astype(jnp.bfloat16)
    sent = pack(hits, (gate_w, up_w, down_w), (gate_scale, up_scale, down_scale))
    received = lax.all_to_all(sent, "wide", split_axis=0, concat_axis=0, tiled=True)
    weights = received.reshape(width, COLUMNS)

    def shift(value, step):
        return lax.ppermute(value, "narrow", [(i, (i + step) % devices) for i in range(devices)])

    mine = jnp.concatenate([tokens, cotangent, rweight], axis=1)
    blocks = [mine] + [shift(mine, s) for s in range(1, devices)]
    places, *gathered = flip(hits, blocks, width, experts)
    terms, act = middle(*gathered, weights)
    back = lax.all_to_all(
        terms.reshape(groups, owner_rows, COLUMNS), "wide", split_axis=0, concat_axis=0, tiled=True
    )
    parts = outputs(act, weights, devices)
    parts = [parts[0]] + [shift(parts[s], devices - s) for s in range(1, devices)]
    total = sum(p.astype(jnp.float32) for p in parts).astype(jnp.bfloat16)
    mixed, token_grad = total[:, :width], total[:, width:]
    gate_grad, up_grad, down_grad = settle(places, back, gate_w)
    return (mixed, token_grad, gate_grad, up_grad, down_grad)


def solution(mesh):
    placed = (
        P(("wide", "narrow"), None),
        P(("wide", "narrow"), None),
        P(("wide", "narrow"), None),
        P(),
        P("wide", "narrow", None),
        P("wide", "narrow", None),
        P("wide", "narrow", None),
        P("wide", None),
        P("wide", None),
        P("wide", None),
        P(("wide", "narrow"), None),
    )
    return jax.shard_map(
        per_device,
        mesh=mesh,
        in_specs=placed,
        out_specs=(
            P(("wide", "narrow"), None),
            P(("wide", "narrow"), None),
            P("wide", "narrow", None),
            P("wide", "narrow", None),
            P("wide", "narrow", None),
        ),
        check_vma=False,
    )
```

```python
import jax
import jax.numpy as jnp
from jax import lax
from jax.experimental import pallas as pl
from jax.experimental.pallas import tpu as pltpu
from jax.sharding import PartitionSpec as P

LANES = 128
MIB = 1024 * 1024
PARTS = 8
STEPS = 4
AHEAD = 6
SIZE = 512
CHUNK = 256

COLUMNS = 896


def lane_index(shape):
    return lax.broadcasted_iota(jnp.int32, shape, len(shape) - 1)


def batched(count, size, load, store):
    @pl.loop(0, count // size)
    def _(i):
        values = [load(i * size + j) for j in range(size)]
        for j in range(size):
            store(i * size + j, values[j])


def pack_kernel(
    hits_hbm,
    gate_hbm,
    up_hbm,
    down_hbm,
    gs_hbm,
    us_hbm,
    ds_hbm,
    out_ref,
    hits_ref,
    stored,
    scales,
    held,
    wide,
    ready,
    in_sem,
    sem,
):
    _, rows, block, experts = stored.shape
    groups = out_ref.shape[0]
    pairs = [(hits_hbm, hits_ref)]
    for m, (w_hbm, s_hbm) in enumerate(((gate_hbm, gs_hbm), (up_hbm, us_hbm), (down_hbm, ds_hbm))):
        pairs += [(s_hbm, scales.at[m]), (w_hbm, stored.at[m])]
    fetches = [pltpu.make_async_copy(*pair, in_sem.at[i]) for i, pair in enumerate(pairs)]
    for copy in fetches:
        copy.start()
    fetches[0].wait()
    for m in range(3):
        fetches[2 * m + 1].wait()
        fetches[2 * m + 2].wait()
        wide[m] = scales[m].astype(jnp.float32)

        def scaled(r, m=m):
            w = (stored[m, r].astype(jnp.float32) * wide[m, pl.ds(r, 1), :]).astype(jnp.bfloat16)
            w = jnp.concatenate([w, jnp.zeros((LANES - block, experts), jnp.bfloat16)], axis=0)
            return w.T.astype(jnp.float32)

        def keep(r, flipped, m=m):
            held[m, pl.ds(r, experts, stride=rows), :] = flipped

        batched(rows, 16, scaled, keep)
    lane = lane_index((rows, LANES))

    def message(g):
        tiles, tail = [], jnp.zeros((rows, LANES), jnp.bfloat16)
        starts = [pl.multiple_of(hits_ref[k, g] * rows, rows) for k in range(3)]
        for m in range(3):
            first, second, third = [held[m, pl.ds(s, rows), :].astype(jnp.bfloat16) for s in starts]
            moved = pltpu.roll(second, 96, 1)
            last = pltpu.roll(third, 64, 1)
            tiles.append(jnp.where(lane < 96, first, moved))
            tiles.append(jnp.where(lane < 64, moved, last))
            rest = last if m == 0 else third if m == 2 else pltpu.roll(third, 96, 1)
            tail = jnp.where((lane >= 32 * m) & (lane < 32 * m + 32), rest, tail)
        return tiles + [tail]

    def emit(g, tiles):
        for q, tile in enumerate(tiles):
            ready[g, :, LANES * q : LANES * q + LANES] = tile

    size = groups // PARTS

    def move(i):
        part = pl.ds(i * size, size)
        return pltpu.make_async_copy(ready.at[part], out_ref.at[part], sem.at[i])

    for i in range(PARTS):
        batched(size, 16, lambda g, i=i: message(i * size + g), lambda g, t, i=i: emit(i * size + g, t))
        move(i).start()
    for i in range(PARTS):
        move(i).wait()


def settle_kernel(
    places_hbm, recv_ref, gate_ref, up_ref, down_ref, places_ref, here, norm, acc, grads, sem, places_sem, out_sem
):
    _, rows, block, experts = grads.shape
    groups = recv_ref.shape[0]
    size = groups // PARTS

    def move(i):
        part = pl.ds(i * size, size)
        return pltpu.make_async_copy(recv_ref.at[part], here.at[part], sem.at[i])

    for i in range(PARTS):
        move(i).start()
    get_places = pltpu.make_async_copy(places_hbm, places_ref, places_sem)
    get_places.start()
    lane = lane_index((rows, LANES))

    def terms(g):
        tail = here[g, :, 768:896]
        out = []
        for m in range(3):
            low = here[g, :, 256 * m : 256 * m + 128]
            high = here[g, :, 256 * m + 128 : 256 * m + 256]
            second = pltpu.roll(jnp.where(lane < 64, high, low), 32, 1)
            if m == 0:
                third = pltpu.roll(jnp.where(lane < 64, tail, high), 64, 1)
            else:
                rest = tail if m == 2 else pltpu.roll(tail, 32, 1)
                third = jnp.where(lane < 64, pltpu.roll(high, 64, 1), rest)
            out.append((low, second, third))
        return out

    def keep(g, out):
        for m in range(3):
            for k in range(3):
                norm[m, 3 * g + k] = out[m][k]

    for i in range(PARTS):
        move(i).wait()
        batched(size, 16, lambda g, i=i: terms(i * size + g), lambda g, t, i=i: keep(i * size + g, t))

    def total(e):
        spots = [places_ref[q, e] for q in range(3)]
        out = []
        for m in range(3):
            a, b, c = [norm[m, s].astype(jnp.float32) for s in spots]
            out.append(a + b + c)
        return out

    def put(e, out):
        for m in range(3):
            acc[m, pl.ds(pl.multiple_of(e * rows, rows), rows), :] = out[m]

    get_places.wait()
    batched(experts, 16, total, put)

    def flipped(r):
        return [acc[m, pl.ds(r, experts, stride=rows), :].astype(jnp.bfloat16).T[:block] for m in range(3)]

    def finish(r, out):
        for m in range(3):
            grads[m, r] = out[m]

    puts = []
    for half in range(2):
        part = pl.ds(half * rows // 2, rows // 2)
        batched(rows // 2, 8, lambda r, h=half: flipped(h * rows // 2 + r), lambda r, out, h=half: finish(h * rows // 2 + r, out))
        for m, ref in enumerate((gate_ref, up_ref, down_ref)):
            puts.append(pltpu.make_async_copy(grads.at[m, part], ref.at[part], out_sem.at[3 * half + m]))
            puts[-1].start()
    for copy in puts:
        copy.wait()


def dot(left, right):
    return lax.dot_general(left, right, (((1,), (0,)), ((), ())), preferred_element_type=jnp.float32)


def dot_t(left, right):
    return lax.dot_general(left, right, (((1,), (1,)), ((), ())), preferred_element_type=jnp.float32)


def middle_kernel(
    x_hbm, dy_hbm, xt_hbm, dyt_hbm, rw_hbm, w_hbm, term_ref, act_ref, x, dy, xt, dyt, rw, w, act, act_rest, ready, pre, rest, sem, flip_sem, out_sem
):
    tok, width = x.shape

    steps = STEPS
    depth = width // steps

    def arriving(i):
        part = pl.ds(i * depth, depth)
        pairs = ((x_hbm.at[:, part], x.at[:, part]), (dy_hbm.at[:, part], dy.at[:, part]), (w_hbm.at[part], w.at[part]))
        return [pltpu.make_async_copy(*pair, sem.at[3 * i + j]) for j, pair in enumerate(pairs)]

    def flipped(i):
        part = pl.ds(i * size, size)
        pairs = ((xt_hbm.at[part], xt.at[part]), (dyt_hbm.at[part], dyt.at[part]))
        return [pltpu.make_async_copy(*pair, flip_sem.at[2 * i + j]) for j, pair in enumerate(pairs)]

    size = SIZE
    waiting = [arriving(i) for i in range(steps)]
    waiting.append([pltpu.make_async_copy(rw_hbm, rw, sem.at[3 * steps])])
    waiting += [flipped(i) for i in range(width // size)]
    for group in waiting[:AHEAD]:
        for copy in group:
            copy.start()
    started = AHEAD
    for i in range(steps):
        for copy in waiting[i]:
            copy.wait()
        for copy in waiting[started] if started < len(waiting) else ():
            copy.start()
        started += 1
        part = pl.ds(i * depth, depth)
        for left, cols in ((x, slice(0, 512)), (dy, slice(512, 768))):
            term = dot(left[:, part], w[part, cols])
            pre[:, cols] = term if i == 0 else pre[:, cols] + term
    for group in waiting[started:]:
        for copy in group:
            copy.start()
    waiting[steps][0].wait()

    def finish(gate, up, back, share):
        sig = jax.nn.sigmoid(gate)
        silu = gate * sig
        weighted = share * silu * up
        d_act = share * back
        d_gate = d_act * up * sig * (1.0 + gate * (1.0 - sig))
        return d_gate, d_act * silu, weighted

    chunk = CHUNK
    lane = lane_index((chunk, LANES))

    def shares(rows):
        share = rw[rows, :].astype(jnp.float32)
        return share[:, 0:1], share[:, 1:2], share[:, 2:3]

    for i in range(tok // chunk):
        rows = pl.ds(i * chunk, chunk)
        one, two, three = shares(rows)
        for h, part in enumerate((jnp.where(lane < 96, one, two), jnp.where(lane < 64, two, three))):
            at = [slice(256 * m + 128 * h, 256 * m + 128 * h + 128) for m in range(3)]
            for span, value in zip(at, finish(*[pre[rows, span] for span in at], part)):
                act[rows, span] = value.astype(jnp.bfloat16)
    rest[:, 0:128] = dot(x[...], w[:, 768:896])
    rest[:, 128:256] = dot(dy[...], w[:, 768:896])
    put_act = [
        pltpu.make_async_copy(act, act_ref.at[:, pl.ds(0, 768)], sem.at[3 * steps + 1]),
        pltpu.make_async_copy(act_rest, act_ref.at[:, pl.ds(768, 256)], sem.at[3 * steps + 2]),
    ]
    put_act[0].start()

    def send(i):
        part = pl.ds(pl.multiple_of(i * size, size), size)
        return pltpu.make_async_copy(ready.at[part], term_ref.at[part], out_sem.at[i])

    for group in waiting[steps + 1 :]:
        for copy in group:
            copy.wait()
    for i in range(tok // chunk):
        rows = pl.ds(i * chunk, chunk)
        three = shares(rows)[2]
        tail_x, tail_dy = rest[rows, 0:128], rest[rows, 128:256]
        d_gate, d_up, weighted = finish(tail_x, pltpu.roll(tail_x, 96, 1), pltpu.roll(tail_dy, 64, 1), three)
        from_x = jnp.where(lane < 32, d_gate, jnp.where(lane < 64, pltpu.roll(d_up, 32, 1), 0.0))
        from_dy = jnp.where((lane >= 64) & (lane < 96), pltpu.roll(weighted, 64, 1), 0.0)
        act_rest[rows, 0:128] = from_x.astype(jnp.bfloat16)
        act_rest[rows, 128:256] = from_dy.astype(jnp.bfloat16)
    for i in range(width // size):
        cols = pl.ds(i * size, size)
        left, right = xt[cols, :], dyt[cols, :]
        ready[cols, 0:512] = dot(left, act[:, 0:512]).astype(jnp.bfloat16)
        ready[cols, 512:768] = dot(right, act[:, 512:768]).astype(jnp.bfloat16)
        tail = dot(left, act_rest[:, 0:128]) + dot(right, act_rest[:, 128:256])
        ready[cols, 768:896] = tail.astype(jnp.bfloat16)
        send(i).start()
        if i == 0:
            put_act[1].start()

    for copy in put_act:
        copy.wait()
    for i in range(width // size):
        send(i).wait()


def out_kernel(act_ref, w_ref, *outs):
    width = w_ref.shape[0]
    size = outs[0].shape[0]

    @pl.loop(0, width // 512)
    def _(i):
        start = pl.multiple_of(i * 512, 512)
        cols = pl.ds(start, 512)
        tail = w_ref[cols, 768:896]
        mixed = dot_t(act_ref[:, 512:768], w_ref[cols, 512:768]) + dot_t(act_ref[:, 896:1024], tail)
        grad = dot_t(act_ref[:, 0:512], w_ref[cols, 0:512]) + dot_t(act_ref[:, 768:896], tail)
        for s, out_ref in enumerate(outs):
            part = slice(s * size, s * size + size)
            out_ref[:, cols] = mixed[part].astype(jnp.bfloat16)
            out_ref[:, pl.ds(pl.multiple_of(start + width, 512), 512)] = grad[part].astype(jnp.bfloat16)


def flip_kernel(hits_ref, *refs):
    *blocks, places_ref, x_ref, dy_ref, xt_ref, dyt_ref, rw_ref, count = refs
    slots, groups = hits_ref.shape
    experts = places_ref.shape[1]
    size = blocks[0].shape[0]
    width = x_ref.shape[1]
    for s, ref in enumerate(blocks):
        rows = pl.ds(s * size, size)
        x_ref[rows, :] = ref[:, 0:width]
        dy_ref[rows, :] = ref[:, width : 2 * width]
        rw_ref[rows, :] = ref[:, 2 * width :]

    @pl.loop(0, width // 512)
    def _(i):
        cols = pl.ds(pl.multiple_of(i * 512, 512), 512)
        xt_ref[cols, :] = x_ref[:, cols].T
        dyt_ref[cols, :] = dy_ref[:, cols].T

    @pl.loop(0, experts)
    def _(e):
        count[e] = 0

    @pl.loop(0, groups)
    def _(g):
        for k in range(slots):
            e = hits_ref[k, g]
            seen = count[e]
            places_ref[seen, e] = slots * g + k
            count[e] = seen + 1


def call(body, outputs, inputs, spaces, out_spaces, scratch=(), limit=16, flops=0):
    moved = sum(a.size * a.dtype.itemsize for a in (*inputs, *outputs))
    return pl.pallas_call(
        body,
        out_shape=outputs,
        in_specs=[pl.BlockSpec(memory_space=s) for s in spaces],
        out_specs=[pl.BlockSpec(memory_space=s) for s in out_spaces],
        scratch_shapes=list(scratch),
        compiler_params=pltpu.CompilerParams(vmem_limit_bytes=limit * MIB),
        cost_estimate=pl.CostEstimate(flops=flops, bytes_accessed=moved, transcendentals=0),
    )(*inputs)


VMEM, SMEM, ANY = pltpu.VMEM, pltpu.SMEM, pl.ANY


def shape(*dims):
    return jax.ShapeDtypeStruct(dims, jnp.bfloat16)


def pack(hits, weights, scales):
    rows, _, experts = weights[0].shape
    groups = hits.shape[1]
    scratch = (
        SMEM(hits.shape, jnp.int32),
        VMEM((3, *weights[0].shape), jnp.bfloat16),
        VMEM((3, rows, experts), jnp.bfloat16),
        VMEM((3, rows * experts, LANES), jnp.float32),
        VMEM((3, rows, experts), jnp.float32),
        VMEM((groups, rows, COLUMNS), jnp.bfloat16),
        pltpu.SemaphoreType.DMA((7,)),
        pltpu.SemaphoreType.DMA((PARTS,)),
    )
    return call(
        pack_kernel,
        [shape(groups, rows, COLUMNS)],
        (hits, *weights, *scales),
        [ANY] * 7,
        [ANY],
        scratch,
        limit=60,
    )[0]


def settle(places, received, like):
    rows, _, experts = like.shape
    groups = received.shape[0]
    scratch = (
        SMEM(places.shape, jnp.int32),
        VMEM((groups, rows, COLUMNS), jnp.bfloat16),
        VMEM((3, 3 * groups, rows, LANES), jnp.bfloat16),
        VMEM((3, experts * rows, LANES), jnp.float32),
        VMEM((3, *like.shape), jnp.bfloat16),
        pltpu.SemaphoreType.DMA((PARTS,)),
        pltpu.SemaphoreType.DMA,
        pltpu.SemaphoreType.DMA((6,)),
    )
    return call(
        settle_kernel, [shape(*like.shape)] * 3, (places, received), [ANY] * 2, [ANY] * 3, scratch, limit=60
    )


def middle(x, dy, xt, dyt, rw, weights):
    tok, width = x.shape
    scratch = (
        *[VMEM(a.shape, jnp.bfloat16) for a in (x, dy, xt, dyt, rw, weights)],
        VMEM((tok, 768), jnp.bfloat16),
        VMEM((tok, 256), jnp.bfloat16),
        VMEM((width, COLUMNS), jnp.bfloat16),
        VMEM((tok, 768), jnp.float32),
        VMEM((tok, 256), jnp.float32),
        pltpu.SemaphoreType.DMA((3 * STEPS + 3,)),
        pltpu.SemaphoreType.DMA((2 * width // SIZE,)),
        pltpu.SemaphoreType.DMA((width // SIZE,)),
    )
    return call(
        middle_kernel,
        [shape(width, COLUMNS), shape(tok, 1024)],
        (x, dy, xt, dyt, rw, weights),
        [ANY] * 6,
        [ANY, ANY],
        scratch,
        limit=60,
        flops=2 * 6 * tok * width * 288,
    )


def outputs(act, weights, devices):
    tok = act.shape[0]
    width = weights.shape[0]
    return call(
        out_kernel,
        [shape(tok // devices, 2 * width)] * devices,
        (act, weights),
        [VMEM] * 2,
        [VMEM] * devices,
        limit=60,
        flops=2 * 3 * tok * width * 288,
    )


def flip(hits, blocks, width, experts):
    tok = blocks[0].shape[0] * len(blocks)
    return call(
        flip_kernel,
        [jax.ShapeDtypeStruct((hits.shape[0], experts), jnp.int32)]
        + [shape(tok, width)] * 2
        + [shape(width, tok)] * 2
        + [shape(tok, LANES)],
        (hits, *blocks),
        [SMEM] + [VMEM] * len(blocks),
        [SMEM] + [VMEM] * 5,
        (SMEM((experts,), jnp.int32),),
        limit=60,
    )


def per_device(
    tokens,
    route_slot,
    route_code,
    group_hits,
    gate_w,
    up_w,
    down_w,
    gate_scale,
    up_scale,
    down_scale,
    cotangent,
):
    hit_count = group_hits.shape[1]
    groups = group_hits.shape[0]
    devices = lax.axis_size("narrow")
    owner_rows, _, experts = gate_w.shape
    width = tokens.shape[1]
    hits = group_hits.T
    codes = route_code.astype(jnp.float32)
    shares = codes / jnp.sum(codes, axis=1, keepdims=True)
    slots = jnp.arange(LANES, dtype=jnp.int32)
    picked = (route_slot[:, :, None] == slots[None, None, :]).astype(jnp.float32)
    rweight = jnp.sum(picked * shares[:, :, None], axis=1).astype(jnp.bfloat16)
    sent = pack(hits, (gate_w, up_w, down_w), (gate_scale, up_scale, down_scale))
    received = lax.all_to_all(sent, "wide", split_axis=0, concat_axis=0, tiled=True)
    weights = received.reshape(width, COLUMNS)

    def shift(value, step):
        return lax.ppermute(value, "narrow", [(i, (i + step) % devices) for i in range(devices)])

    mine = jnp.concatenate([tokens, cotangent, rweight], axis=1)
    blocks = [mine] + [shift(mine, s) for s in range(1, devices)]
    places, *gathered = flip(hits, blocks, width, experts)
    terms, act = middle(*gathered, weights)
    back = lax.all_to_all(
        terms.reshape(groups, owner_rows, COLUMNS), "wide", split_axis=0, concat_axis=0, tiled=True
    )
    parts = outputs(act, weights, devices)
    parts = [parts[0]] + [shift(parts[s], devices - s) for s in range(1, devices)]
    total = sum(p.astype(jnp.float32) for p in parts).astype(jnp.bfloat16)
    mixed, token_grad = total[:, :width], total[:, width:]
    gate_grad, up_grad, down_grad = settle(places, back, gate_w)
    return (mixed, token_grad, gate_grad, up_grad, down_grad)


def solution(mesh):
    placed = (
        P(("wide", "narrow"), None),
        P(("wide", "narrow"), None),
        P(("wide", "narrow"), None),
        P(),
        P("wide", "narrow", None),
        P("wide", "narrow", None),
        P("wide", "narrow", None),
        P("wide", None),
        P("wide", None),
        P("wide", None),
        P(("wide", "narrow"), None),
    )
    return jax.shard_map(
        per_device,
        mesh=mesh,
        in_specs=placed,
        out_specs=(
            P(("wide", "narrow"), None),
            P(("wide", "narrow"), None),
            P("wide", "narrow", None),
            P("wide", "narrow", None),
            P("wide", "narrow", None),
        ),
        check_vma=False,
    )
```

```python
import jax
import jax.numpy as jnp
from jax import lax
from jax.experimental import pallas as pl
from jax.experimental.pallas import tpu as pltpu
from jax.sharding import PartitionSpec as P

LANES = 128
MIB = 1024 * 1024
PARTS = 8
STEPS = 4
AHEAD = 6
SIZE = 512
CHUNK = 256

COLUMNS = 896


def lane_index(shape):
    return lax.broadcasted_iota(jnp.int32, shape, len(shape) - 1)


def batched(count, size, load, store):
    @pl.loop(0, count // size)
    def _(i):
        values = [load(i * size + j) for j in range(size)]
        for j in range(size):
            store(i * size + j, values[j])


def pack_kernel(
    hits_hbm,
    gate_hbm,
    up_hbm,
    down_hbm,
    gs_hbm,
    us_hbm,
    ds_hbm,
    out_ref,
    hits_ref,
    stored,
    scales,
    held,
    wide,
    ready,
    in_sem,
    sem,
):
    _, rows, block, experts = stored.shape
    groups = out_ref.shape[0]
    pairs = [(hits_hbm, hits_ref)]
    for m, (w_hbm, s_hbm) in enumerate(((gate_hbm, gs_hbm), (up_hbm, us_hbm), (down_hbm, ds_hbm))):
        pairs += [(s_hbm, scales.at[m]), (w_hbm, stored.at[m])]
    fetches = [pltpu.make_async_copy(*pair, in_sem.at[i]) for i, pair in enumerate(pairs)]
    for copy in fetches:
        copy.start()
    fetches[0].wait()
    for m in range(3):
        fetches[2 * m + 1].wait()
        fetches[2 * m + 2].wait()
        wide[m] = scales[m].astype(jnp.float32)

        def scaled(r, m=m):
            w = (stored[m, r].astype(jnp.float32) * wide[m, pl.ds(r, 1), :]).astype(jnp.bfloat16)
            w = jnp.concatenate([w, jnp.zeros((LANES - block, experts), jnp.bfloat16)], axis=0)
            return w.T.astype(jnp.float32)

        def keep(r, flipped, m=m):
            held[m, pl.ds(r, experts, stride=rows), :] = flipped

        batched(rows, 16, scaled, keep)
    lane = lane_index((rows, LANES))

    def message(g):
        tiles, tail = [], jnp.zeros((rows, LANES), jnp.bfloat16)
        starts = [pl.multiple_of(hits_ref[k, g] * rows, rows) for k in range(3)]
        for m in range(3):
            first, second, third = [held[m, pl.ds(s, rows), :].astype(jnp.bfloat16) for s in starts]
            moved = pltpu.roll(second, 96, 1)
            last = pltpu.roll(third, 64, 1)
            tiles.append(jnp.where(lane < 96, first, moved))
            tiles.append(jnp.where(lane < 64, moved, last))
            rest = last if m == 0 else third if m == 2 else pltpu.roll(third, 96, 1)
            tail = jnp.where((lane >= 32 * m) & (lane < 32 * m + 32), rest, tail)
        return tiles + [tail]

    def emit(g, tiles):
        for q, tile in enumerate(tiles):
            ready[g, :, LANES * q : LANES * q + LANES] = tile

    size = groups // PARTS

    def move(i):
        part = pl.ds(i * size, size)
        return pltpu.make_async_copy(ready.at[part], out_ref.at[part], sem.at[i])

    for i in range(PARTS):
        batched(size, 16, lambda g, i=i: message(i * size + g), lambda g, t, i=i: emit(i * size + g, t))
        move(i).start()
    for i in range(PARTS):
        move(i).wait()


def settle_kernel(
    places_hbm, recv_ref, gate_ref, up_ref, down_ref, places_ref, here, norm, acc, grads, sem, places_sem, out_sem
):
    _, rows, block, experts = grads.shape
    groups = recv_ref.shape[0]
    size = groups // PARTS

    def move(i):
        part = pl.ds(i * size, size)
        return pltpu.make_async_copy(recv_ref.at[part], here.at[part], sem.at[i])

    for i in range(PARTS):
        move(i).start()
    get_places = pltpu.make_async_copy(places_hbm, places_ref, places_sem)
    get_places.start()
    lane = lane_index((rows, LANES))

    def terms(g):
        tail = here[g, :, 768:896]
        out = []
        for m in range(3):
            low = here[g, :, 256 * m : 256 * m + 128]
            high = here[g, :, 256 * m + 128 : 256 * m + 256]
            second = pltpu.roll(jnp.where(lane < 64, high, low), 32, 1)
            if m == 0:
                third = pltpu.roll(jnp.where(lane < 64, tail, high), 64, 1)
            else:
                rest = tail if m == 2 else pltpu.roll(tail, 32, 1)
                third = jnp.where(lane < 64, pltpu.roll(high, 64, 1), rest)
            out.append((low, second, third))
        return out

    def keep(g, out):
        for m in range(3):
            for k in range(3):
                norm[m, 3 * g + k] = out[m][k]

    for i in range(PARTS):
        move(i).wait()
        batched(size, 16, lambda g, i=i: terms(i * size + g), lambda g, t, i=i: keep(i * size + g, t))

    def total(e):
        spots = [places_ref[q, e] for q in range(3)]
        out = []
        for m in range(3):
            a, b, c = [norm[m, s].astype(jnp.float32) for s in spots]
            out.append(a + b + c)
        return out

    def put(e, out):
        for m in range(3):
            acc[m, pl.ds(pl.multiple_of(e * rows, rows), rows), :] = out[m]

    get_places.wait()
    batched(experts, 16, total, put)

    def flipped(r):
        return [acc[m, pl.ds(r, experts, stride=rows), :].astype(jnp.bfloat16).T[:block] for m in range(3)]

    def finish(r, out):
        for m in range(3):
            grads[m, r] = out[m]

    puts = []
    for half in range(4):
        part = pl.ds(half * rows // 4, rows // 4)
        batched(rows // 4, 4, lambda r, h=half: flipped(h * rows // 4 + r), lambda r, out, h=half: finish(h * rows // 4 + r, out))
        for m, ref in enumerate((gate_ref, up_ref, down_ref)):
            puts.append(pltpu.make_async_copy(grads.at[m, part], ref.at[part], out_sem.at[3 * half + m]))
            puts[-1].start()
    for copy in puts:
        copy.wait()


def dot(left, right):
    return lax.dot_general(left, right, (((1,), (0,)), ((), ())), preferred_element_type=jnp.float32)


def dot_t(left, right):
    return lax.dot_general(left, right, (((1,), (1,)), ((), ())), preferred_element_type=jnp.float32)


def middle_kernel(
    x_hbm, dy_hbm, xt_hbm, dyt_hbm, rw_hbm, w_hbm, term_ref, act_ref, x, dy, flips, rw, w, act, act_rest, ready, pre, rest, sem, flip_sem, out_sem
):
    tok, width = x.shape

    steps = STEPS
    depth = width // steps

    def arriving(i):
        part = pl.ds(i * depth, depth)
        pairs = ((x_hbm.at[:, part], x.at[:, part]), (dy_hbm.at[:, part], dy.at[:, part]), (w_hbm.at[part], w.at[part]))
        return [pltpu.make_async_copy(*pair, sem.at[3 * i + j]) for j, pair in enumerate(pairs)]

    def flipped(i):
        part = pl.ds(i * size, size)
        pairs = ((xt_hbm.at[part], flips.at[part, pl.ds(0, tok)]), (dyt_hbm.at[part], flips.at[part, pl.ds(tok, tok)]))
        return [pltpu.make_async_copy(*pair, flip_sem.at[2 * i + j]) for j, pair in enumerate(pairs)]

    size = SIZE
    waiting = [arriving(i) for i in range(steps)]
    waiting.append([pltpu.make_async_copy(rw_hbm, rw, sem.at[3 * steps])])
    waiting += [flipped(i) for i in range(width // size)]
    for group in waiting[:AHEAD]:
        for copy in group:
            copy.start()
    started = AHEAD
    for i in range(steps):
        for copy in waiting[i]:
            copy.wait()
        for copy in waiting[started] if started < len(waiting) else ():
            copy.start()
        started += 1
        part = pl.ds(i * depth, depth)
        for left, cols in ((x, slice(0, 512)), (dy, slice(512, 768))):
            term = dot(left[:, part], w[part, cols])
            pre[:, cols] = term if i == 0 else pre[:, cols] + term
    for group in waiting[started:]:
        for copy in group:
            copy.start()
    waiting[steps][0].wait()

    def finish(gate, up, back, share):
        sig = jax.nn.sigmoid(gate)
        silu = gate * sig
        weighted = share * silu * up
        d_act = share * back
        d_gate = d_act * up * sig * (1.0 + gate * (1.0 - sig))
        return d_gate, d_act * silu, weighted

    chunk = CHUNK
    lane = lane_index((chunk, LANES))

    def shares(rows):
        share = rw[rows, :].astype(jnp.float32)
        return share[:, 0:1], share[:, 1:2], share[:, 2:3]

    for i in range(tok // chunk):
        rows = pl.ds(i * chunk, chunk)
        one, two, three = shares(rows)
        for h, part in enumerate((jnp.where(lane < 96, one, two), jnp.where(lane < 64, two, three))):
            at = [slice(256 * m + 128 * h, 256 * m + 128 * h + 128) for m in range(3)]
            for span, value in zip(at, finish(*[pre[rows, span] for span in at], part)):
                act[rows, span] = value.astype(jnp.bfloat16)
    rest[:, 0:128] = dot(x[...], w[:, 768:896])
    rest[:, 128:256] = dot(dy[...], w[:, 768:896])
    put_act = [
        pltpu.make_async_copy(act, act_ref.at[:, pl.ds(0, 768)], sem.at[3 * steps + 1]),
        pltpu.make_async_copy(act_rest.at[pl.ds(0, tok)], act_ref.at[:, pl.ds(768, 128)], sem.at[3 * steps + 2]),
        pltpu.make_async_copy(act_rest.at[pl.ds(tok, tok)], act_ref.at[:, pl.ds(896, 128)], sem.at[3 * steps + 3]),
    ]
    put_act[0].start()

    def send(i):
        part = pl.ds(pl.multiple_of(i * size, size), size)
        return pltpu.make_async_copy(ready.at[part], term_ref.at[part], out_sem.at[i])

    for group in waiting[steps + 1 :]:
        for copy in group:
            copy.wait()
    for i in range(tok // chunk):
        rows = pl.ds(i * chunk, chunk)
        three = shares(rows)[2]
        tail_x, tail_dy = rest[rows, 0:128], rest[rows, 128:256]
        d_gate, d_up, weighted = finish(tail_x, pltpu.roll(tail_x, 96, 1), pltpu.roll(tail_dy, 64, 1), three)
        from_x = jnp.where(lane < 32, d_gate, jnp.where(lane < 64, pltpu.roll(d_up, 32, 1), 0.0))
        from_dy = jnp.where((lane >= 64) & (lane < 96), pltpu.roll(weighted, 64, 1), 0.0)
        act_rest[rows, :] = from_x.astype(jnp.bfloat16)
        act_rest[pl.ds(tok + i * chunk, chunk), :] = from_dy.astype(jnp.bfloat16)
    for i in range(width // size):
        cols = pl.ds(i * size, size)
        left, right = flips[cols, 0:tok], flips[cols, tok : 2 * tok]
        ready[cols, 0:512] = dot(left, act[:, 0:512]).astype(jnp.bfloat16)
        ready[cols, 512:768] = dot(right, act[:, 512:768]).astype(jnp.bfloat16)
        tail = dot(flips[cols, :], act_rest[...])
        ready[cols, 768:896] = tail.astype(jnp.bfloat16)
        send(i).start()
        if i == 0:
            put_act[1].start()
            put_act[2].start()

    for copy in put_act:
        copy.wait()
    for i in range(width // size):
        send(i).wait()


def out_kernel(act_ref, w_ref, *outs):
    width = w_ref.shape[0]
    size = outs[0].shape[0]

    @pl.loop(0, width // 512)
    def _(i):
        start = pl.multiple_of(i * 512, 512)
        cols = pl.ds(start, 512)
        tail = w_ref[cols, 768:896]
        mixed = dot_t(act_ref[:, 512:768], w_ref[cols, 512:768]) + dot_t(act_ref[:, 896:1024], tail)
        grad = dot_t(act_ref[:, 0:512], w_ref[cols, 0:512]) + dot_t(act_ref[:, 768:896], tail)
        for s, out_ref in enumerate(outs):
            part = slice(s * size, s * size + size)
            out_ref[:, cols] = mixed[part].astype(jnp.bfloat16)
            out_ref[:, pl.ds(pl.multiple_of(start + width, 512), 512)] = grad[part].astype(jnp.bfloat16)


def flip_kernel(hits_ref, *refs):
    *blocks, places_ref, x_ref, dy_ref, xt_ref, dyt_ref, rw_ref, count = refs
    slots, groups = hits_ref.shape
    experts = places_ref.shape[1]
    size = blocks[0].shape[0]
    width = x_ref.shape[1]
    for s, ref in enumerate(blocks):
        rows = pl.ds(s * size, size)
        x_ref[rows, :] = ref[:, 0:width]
        dy_ref[rows, :] = ref[:, width : 2 * width]
        rw_ref[rows, :] = ref[:, 2 * width :]

    @pl.loop(0, width // 512)
    def _(i):
        cols = pl.ds(pl.multiple_of(i * 512, 512), 512)
        xt_ref[cols, :] = x_ref[:, cols].T
        dyt_ref[cols, :] = dy_ref[:, cols].T

    @pl.loop(0, experts)
    def _(e):
        count[e] = 0

    @pl.loop(0, groups)
    def _(g):
        for k in range(slots):
            e = hits_ref[k, g]
            seen = count[e]
            places_ref[seen, e] = slots * g + k
            count[e] = seen + 1


def call(body, outputs, inputs, spaces, out_spaces, scratch=(), limit=16, flops=0):
    moved = sum(a.size * a.dtype.itemsize for a in (*inputs, *outputs))
    return pl.pallas_call(
        body,
        out_shape=outputs,
        in_specs=[pl.BlockSpec(memory_space=s) for s in spaces],
        out_specs=[pl.BlockSpec(memory_space=s) for s in out_spaces],
        scratch_shapes=list(scratch),
        compiler_params=pltpu.CompilerParams(vmem_limit_bytes=limit * MIB),
        cost_estimate=pl.CostEstimate(flops=flops, bytes_accessed=moved, transcendentals=0),
    )(*inputs)


VMEM, SMEM, ANY = pltpu.VMEM, pltpu.SMEM, pl.ANY


def shape(*dims):
    return jax.ShapeDtypeStruct(dims, jnp.bfloat16)


def pack(hits, weights, scales):
    rows, _, experts = weights[0].shape
    groups = hits.shape[1]
    scratch = (
        SMEM(hits.shape, jnp.int32),
        VMEM((3, *weights[0].shape), jnp.bfloat16),
        VMEM((3, rows, experts), jnp.bfloat16),
        VMEM((3, rows * experts, LANES), jnp.float32),
        VMEM((3, rows, experts), jnp.float32),
        VMEM((groups, rows, COLUMNS), jnp.bfloat16),
        pltpu.SemaphoreType.DMA((7,)),
        pltpu.SemaphoreType.DMA((PARTS,)),
    )
    return call(
        pack_kernel,
        [shape(groups, rows, COLUMNS)],
        (hits, *weights, *scales),
        [ANY] * 7,
        [ANY],
        scratch,
        limit=60,
    )[0]


def settle(places, received, like):
    rows, _, experts = like.shape
    groups = received.shape[0]
    scratch = (
        SMEM(places.shape, jnp.int32),
        VMEM((groups, rows, COLUMNS), jnp.bfloat16),
        VMEM((3, 3 * groups, rows, LANES), jnp.bfloat16),
        VMEM((3, experts * rows, LANES), jnp.float32),
        VMEM((3, *like.shape), jnp.bfloat16),
        pltpu.SemaphoreType.DMA((PARTS,)),
        pltpu.SemaphoreType.DMA,
        pltpu.SemaphoreType.DMA((12,)),
    )
    return call(
        settle_kernel, [shape(*like.shape)] * 3, (places, received), [ANY] * 2, [ANY] * 3, scratch, limit=60
    )


def middle(x, dy, xt, dyt, rw, weights):
    tok, width = x.shape
    scratch = (
        *[VMEM(a.shape, jnp.bfloat16) for a in (x, dy)],
        VMEM((width, 2 * tok), jnp.bfloat16),
        *[VMEM(a.shape, jnp.bfloat16) for a in (rw, weights)],
        VMEM((tok, 768), jnp.bfloat16),
        VMEM((2 * tok, 128), jnp.bfloat16),
        VMEM((width, COLUMNS), jnp.bfloat16),
        VMEM((tok, 768), jnp.float32),
        VMEM((tok, 256), jnp.float32),
        pltpu.SemaphoreType.DMA((3 * STEPS + 4,)),
        pltpu.SemaphoreType.DMA((2 * width // SIZE,)),
        pltpu.SemaphoreType.DMA((width // SIZE,)),
    )
    return call(
        middle_kernel,
        [shape(width, COLUMNS), shape(tok, 1024)],
        (x, dy, xt, dyt, rw, weights),
        [ANY] * 6,
        [ANY, ANY],
        scratch,
        limit=60,
        flops=2 * 6 * tok * width * 288,
    )


def outputs(act, weights, devices):
    tok = act.shape[0]
    width = weights.shape[0]
    return call(
        out_kernel,
        [shape(tok // devices, 2 * width)] * devices,
        (act, weights),
        [VMEM] * 2,
        [VMEM] * devices,
        limit=60,
        flops=2 * 3 * tok * width * 288,
    )


def flip(hits, blocks, width, experts):
    tok = blocks[0].shape[0] * len(blocks)
    return call(
        flip_kernel,
        [jax.ShapeDtypeStruct((hits.shape[0], experts), jnp.int32)]
        + [shape(tok, width)] * 2
        + [shape(width, tok)] * 2
        + [shape(tok, LANES)],
        (hits, *blocks),
        [SMEM] + [VMEM] * len(blocks),
        [SMEM] + [VMEM] * 5,
        (SMEM((experts,), jnp.int32),),
        limit=60,
    )


def per_device(
    tokens,
    route_slot,
    route_code,
    group_hits,
    gate_w,
    up_w,
    down_w,
    gate_scale,
    up_scale,
    down_scale,
    cotangent,
):
    hit_count = group_hits.shape[1]
    groups = group_hits.shape[0]
    devices = lax.axis_size("narrow")
    owner_rows, _, experts = gate_w.shape
    width = tokens.shape[1]
    hits = group_hits.T
    codes = route_code.astype(jnp.float32)
    shares = codes / jnp.sum(codes, axis=1, keepdims=True)
    slots = jnp.arange(LANES, dtype=jnp.int32)
    picked = (route_slot[:, :, None] == slots[None, None, :]).astype(jnp.float32)
    rweight = jnp.sum(picked * shares[:, :, None], axis=1).astype(jnp.bfloat16)
    sent = pack(hits, (gate_w, up_w, down_w), (gate_scale, up_scale, down_scale))
    received = lax.all_to_all(sent, "wide", split_axis=0, concat_axis=0, tiled=True)
    weights = received.reshape(width, COLUMNS)

    def shift(value, step):
        return lax.ppermute(value, "narrow", [(i, (i + step) % devices) for i in range(devices)])

    mine = jnp.concatenate([tokens, cotangent, rweight], axis=1)
    blocks = [mine] + [shift(mine, s) for s in range(1, devices)]
    places, *gathered = flip(hits, blocks, width, experts)
    terms, act = middle(*gathered, weights)
    back = lax.all_to_all(
        terms.reshape(groups, owner_rows, COLUMNS), "wide", split_axis=0, concat_axis=0, tiled=True
    )
    parts = outputs(act, weights, devices)
    parts = [parts[0]] + [shift(parts[s], devices - s) for s in range(1, devices)]
    total = sum(p.astype(jnp.float32) for p in parts).astype(jnp.bfloat16)
    mixed, token_grad = total[:, :width], total[:, width:]
    gate_grad, up_grad, down_grad = settle(places, back, gate_w)
    return (mixed, token_grad, gate_grad, up_grad, down_grad)


def solution(mesh):
    placed = (
        P(("wide", "narrow"), None),
        P(("wide", "narrow"), None),
        P(("wide", "narrow"), None),
        P(),
        P("wide", "narrow", None),
        P("wide", "narrow", None),
        P("wide", "narrow", None),
        P("wide", None),
        P("wide", None),
        P("wide", None),
        P(("wide", "narrow"), None),
    )
    return jax.shard_map(
        per_device,
        mesh=mesh,
        in_specs=placed,
        out_specs=(
            P(("wide", "narrow"), None),
            P(("wide", "narrow"), None),
            P("wide", "narrow", None),
            P("wide", "narrow", None),
            P("wide", "narrow", None),
        ),
        check_vma=False,
    )
```
